256 devices in a mesh: section: 16 (over z_hi, y), seq: 16 (over x, z_lo, core).
Axes of the slice: x: 4, y: 4, z: 8 (z_hi: 4, z_lo: 2; z = z_hi * 2 + z_lo), core: 2. Of those that a mesh axis runs over, the one named last changes fastest.
Arguments:
- queries: bfloat16 [16, 1024, 2048], P('section', 'seq'), may hold values from -6 to 6
- out_grad: bfloat16 [16, 1024, 2048], P('section', 'seq'), may hold values from -96 to 96
- keys: bfloat16 [16, 2048, 2048], P('section', 'seq'), may hold values from -6 to 6
- values: bfloat16 [16, 2048, 2048], P('section', 'seq'), may hold values from -6 to 6
- key_weight: bfloat16 [16, 4096, 2048], P('section', 'seq'), may hold values from -0.125 to 0.125
- value_weight: bfloat16 [16, 4096, 2048], P('section', 'seq'), may hold values from -0.125 to 0.125
- owner: int32 [1], replicated, may hold values from 0 to 15
Outputs:
- enc_grad: bfloat16 [16, 2048, 4096], P('section', None, 'seq')
The draws below stay inside these ranges and needn't reach their ends.
All inputs are finite; a program needn't handle non-finite values.
Results may differ from the reference program's by a relative error of at most 0.012.
Values may be sent and summed in bfloat16 or wider, within the bound.
No kernel may reach another device: no remote copies, remote signals or barrier semaphores. Data moves between devices by JAX's collectives and lax.ppermute only.
A program may use at most 128 MiB of HBM per device.

```python
import jax
import jax.numpy as jnp
from jax import lax

D = 4096
HEADS = 8
HEAD = 256
ATTN_WIDTH = 2048
SOURCE = 2048
TARGET = 1024
N_SECTION = 16


def draw_queries(key, part):
    base_key = jax.random.fold_in(key, 11)
    return jnp.clip(jax.random.normal(base_key, (N_SECTION, TARGET, ATTN_WIDTH), jnp.float32), -6.0, 6.0).astype(jnp.bfloat16)


def draw_keys(key, part):
    base_key = jax.random.fold_in(key, 23)
    return jnp.clip(jax.random.normal(base_key, (N_SECTION, SOURCE, ATTN_WIDTH), jnp.float32), -6.0, 6.0).astype(jnp.bfloat16)


def shard_levels(own_key, shape, cuts, smallest, largest):
    def one(position, parts):
        draws = jax.random.uniform(jax.random.fold_in(jax.random.fold_in(own_key, 6), position), (parts,), jnp.float32, smallest / len(cuts), largest / len(cuts))
        return jnp.repeat(jnp.exp(draws), shape[position] // parts).reshape((-1,) + (1,) * (len(shape) - position - 1))

    loudness = one(*cuts[0])
    for cut in cuts[1:]:
        loudness = loudness * one(*cut)
    return loudness


def normal_values(own_key, extent, scale, bound, cuts=(), held_as=jnp.bfloat16):
    entries = jax.random.normal(own_key, extent, jnp.float32) * scale
    if len(cuts) > 0:
        entries = shard_levels(own_key, extent, cuts, -0.22, 0.18) * entries
    return jnp.clip(entries, min=-bound, max=bound).astype(held_as)


def setup_inputs(seed: int = 0) -> dict:
    splits = jax.random.split(jax.random.key(seed), 8)
    queries = draw_queries(jax.random.fold_in(splits[7], 71), 0)
    out_grad = normal_values(splits[1], (N_SECTION, TARGET, ATTN_WIDTH), 16.0, 96.0, ((0, 16), (1, 16)))
    keys = draw_keys(jax.random.fold_in(splits[7], 71), 0)
    values = normal_values(splits[3], (N_SECTION, SOURCE, ATTN_WIDTH), 1.0, 6.0, ((0, 16), (1, 16)))
    key_weight = normal_values(splits[4], (N_SECTION, D, ATTN_WIDTH), ATTN_WIDTH ** -0.5, 0.125, ((0, 16), (1, 16)))
    value_weight = normal_values(splits[5], (N_SECTION, D, ATTN_WIDTH), ATTN_WIDTH ** -0.5, 0.125, ((0, 16), (1, 16)))
    owner = jax.random.randint(splits[6], (1,), 0, N_SECTION).astype(jnp.int32)
    return dict(queries=queries, out_grad=out_grad, keys=keys, values=values, key_weight=key_weight, value_weight=value_weight, owner=owner)


def head_grads(query_head, grad_head, key_head, value_head):
    score_scale = HEAD ** -0.5
    scores = jnp.dot(query_head, key_head.T, preferred_element_type=jnp.float32) * score_scale
    row_peak = jnp.max(scores, axis=1, keepdims=True)
    lse = row_peak + jnp.log(jnp.sum(jnp.exp(scores - row_peak), axis=1, keepdims=True))
    probs = jnp.exp(scores - lse)
    grad_probs = jnp.dot(grad_head, value_head.T, preferred_element_type=jnp.float32)
    row_delta = jnp.sum(probs * grad_probs, axis=1, keepdims=True)
    grad_scores = (probs * (grad_probs - row_delta)).astype(jnp.bfloat16)
    probs_low = probs.astype(jnp.bfloat16)
    value_grad = jnp.dot(probs_low.T, grad_head, preferred_element_type=jnp.float32).astype(jnp.bfloat16)
    key_grad = (jnp.dot(grad_scores.T, query_head, preferred_element_type=jnp.float32) * score_scale).astype(jnp.bfloat16)
    return key_grad, value_grad


def split_heads(matrix):
    return matrix.reshape(matrix.shape[0], HEADS, HEAD).transpose(1, 0, 2)


def join_heads(stacked):
    return stacked.transpose(1, 0, 2).reshape(stacked.shape[1], HEADS * HEAD)


def section_partial(query_rows, grad_rows, key_rows, value_rows, key_proj, value_proj):
    def one_head(head_items):
        return head_grads(head_items[0], head_items[1], head_items[2], head_items[3])

    key_grad, value_grad = lax.map(one_head, (split_heads(query_rows), split_heads(grad_rows), split_heads(key_rows), split_heads(value_rows)))
    key_grad = join_heads(key_grad)
    value_grad = join_heads(value_grad)
    return jnp.dot(key_grad, key_proj.T, preferred_element_type=jnp.float32) + jnp.dot(value_grad, value_proj.T, preferred_element_type=jnp.float32)


def reference(queries, out_grad, keys, values, key_weight, value_weight, owner):
    def step(running, section_items):
        return running + section_partial(*section_items), None

    summed, _ = lax.scan(step, jnp.zeros((SOURCE, D), jnp.float32), (queries, out_grad, keys, values, key_weight, value_weight))
    chosen = (jnp.arange(N_SECTION, dtype=jnp.int32) == owner[0])[:, None, None]
    return jnp.where(chosen, summed.astype(jnp.bfloat16)[None], jnp.zeros((), jnp.bfloat16)).astype(jnp.bfloat16)
```

```python
import jax
import jax.numpy as jnp
from jax import lax
from jax.experimental import pallas as pl
from jax.experimental.pallas import tpu as pltpu
from jax.sharding import PartitionSpec as P

HEAD = 256
PAIR = 512
SCALE = HEAD ** -0.5
CHUNKS = 2
F32 = jnp.float32
BF16 = jnp.bfloat16
NT = (((1,), (1,)), ((), ()))
NN = (((1,), (0,)), ((), ()))


def seq_moves(dx, dz, dc):
    pairs = []
    for x in range(4):
        for z in range(2):
            for c in range(2):
                pairs.append((x * 4 + z * 2 + c, ((x + dx) % 4) * 4 + ((z + dz) % 2) * 2 + (c + dc) % 2))
    return pairs


def section_moves(dh, dy):
    return [(h * 4 + y, ((h + dh) % 4) * 4 + (y + dy) % 4) for h in range(4) for y in range(4)]


def along_seq(value, dx=0, dz=0, dc=0):
    return lax.ppermute(value, "seq", seq_moves(dx, dz, dc))


def along_section(value, dh=0, dy=0):
    return lax.ppermute(value, "section", section_moves(dh, dy))


def dot(a, b, dims):
    return lax.dot_general(a, b, dims, preferred_element_type=F32)


def stats_kernel(q_ref, g_ref, k_ref, v_ref, out_ref):
    keys = k_ref.shape[0]
    queries = q_ref.shape[0]
    out_ref[...] = jnp.zeros_like(out_ref)
    for h in range(2):
        hc = pl.ds(h * HEAD, HEAD)
        for j in range(queries // 256):
            rows = pl.ds(j * 256, 256)
            s = dot(k_ref[:, hc], q_ref[rows, hc], NT) * SCALE
            gp = dot(v_ref[:, hc], g_ref[rows, hc], NT)
            peak = jnp.max(s, axis=0, keepdims=True)
            p = jnp.exp(s - peak)
            out_ref[pl.ds(h * 4, 1), rows] = peak
            out_ref[pl.ds(h * 4 + 1, 1), rows] = jnp.sum(p, axis=0, keepdims=True)
            out_ref[pl.ds(h * 4 + 2, 1), rows] = jnp.sum(p * gp, axis=0, keepdims=True)


def stats(q, g, k, v):
    return pl.pallas_call(
        stats_kernel,
        out_shape=jax.ShapeDtypeStruct((8, q.shape[0]), F32),
        in_specs=[pl.BlockSpec(memory_space=pltpu.VMEM)] * 4,
        out_specs=pl.BlockSpec(memory_space=pltpu.VMEM),
        compiler_params=pltpu.CompilerParams(vmem_limit_bytes=24 * 2**20),
        cost_estimate=pl.CostEstimate(flops=2 * 10**9, bytes_accessed=2**22, transcendentals=2**20),
        name="stats",
    )(q, g, k, v)


def grads_kernel(x_ref, s0, s1, s2, s3, q_ref, g_ref, k_ref, v_ref, a_ref, b_ref, p_s, d_s):
    queries = q_ref.shape[0]
    keys = k_ref.shape[0]
    block = keys // 4
    x = x_ref[0]
    parts = [s0, s1, s2, s3]
    for h in range(2):
        hc = pl.ds(h * HEAD, HEAD)
        for j in range(queries // 256):
            rows = pl.ds(j * 256, 256)
            spots = [pl.ds((j ^ flip) * 256, 256) for flip in (0, 2, 1, 3)]
            peaks = [s[pl.ds(h * 4, 1), spot] for s, spot in zip(parts, spots)]
            peak = jnp.maximum(jnp.maximum(peaks[0], peaks[1]), jnp.maximum(peaks[2], peaks[3]))
            total = jnp.zeros_like(peak)
            weighted = jnp.zeros_like(peak)
            for s, spot, own in zip(parts, spots, peaks):
                factor = jnp.exp(own - peak)
                total += s[pl.ds(h * 4 + 1, 1), spot] * factor
                weighted += s[pl.ds(h * 4 + 2, 1), spot] * factor
            lse = peak + jnp.log(total)
            delta = weighted / total
            s = dot(k_ref[:, hc], q_ref[rows, hc], NT) * SCALE
            gp = dot(v_ref[:, hc], g_ref[rows, hc], NT)
            p = jnp.exp(s - lse)
            p_s[:, rows] = p.astype(BF16)
            d_s[:, rows] = (p * (gp - delta)).astype(BF16)
        kg = (dot(d_s[...], q_ref[:, hc], NN) * SCALE).astype(BF16)
        vg = dot(p_s[...], g_ref[:, hc], NN).astype(BF16)
        for d in range(4):
            at = lax.rem(x - d + 4, 4)
            for half, ref in enumerate((a_ref, b_ref)):
                @pl.when(lax.div(at, 2) == half)
                def _():
                    rows = pl.ds(pl.multiple_of(lax.rem(at, 2) * block, block), block)
                    ref[rows, pl.ds(h * HEAD, HEAD)] = kg[d * block:(d + 1) * block]
                    ref[rows, pl.ds(PAIR + h * HEAD, HEAD)] = vg[d * block:(d + 1) * block]


def grads(x, parts, q, g, k, v):
    keys, queries = k.shape[0], q.shape[0]
    half = jax.ShapeDtypeStruct((keys // 2, 2 * PAIR), BF16)
    return pl.pallas_call(
        grads_kernel,
        out_shape=(half, half),
        in_specs=[pl.BlockSpec(memory_space=pltpu.SMEM)] + [pl.BlockSpec(memory_space=pltpu.VMEM)] * 8,
        out_specs=(pl.BlockSpec(memory_space=pltpu.VMEM),) * 2,
        scratch_shapes=[pltpu.VMEM((keys, queries), BF16)] * 2,
        compiler_params=pltpu.CompilerParams(vmem_limit_bytes=24 * 2**20),
        cost_estimate=pl.CostEstimate(flops=2 * 10**9, bytes_accessed=2**22, transcendentals=2**19),
        name="grads",
    )(x, *parts, q, g, k, v)


def project_kernel(x_ref, *refs):
    blocks, weights, out_ref = refs[:8], refs[8:16], refs[16]
    rows = blocks[0].shape[0]
    x = x_ref[0]
    for half in range(2):
        for w in range(4):
            acc = None
            for d in range(4):
                cols = pl.ds(pl.multiple_of(lax.rem(x - d + 4, 4) * PAIR, PAIR), PAIR)
                block = blocks[2 * d + half]
                for kind in range(2):
                    term = dot(block[:, pl.ds(kind * PAIR, PAIR)], weights[2 * w + kind][:, cols], NT)
                    acc = term if acc is None else acc + term
            out_ref[pl.ds(half * rows, rows), pl.ds(w * 256, 256)] = acc.astype(BF16)


def project(x, blocks, weights):
    rows = 2 * blocks[0].shape[0]
    return pl.pallas_call(
        project_kernel,
        out_shape=jax.ShapeDtypeStruct((rows, 1024), BF16),
        in_specs=[pl.BlockSpec(memory_space=pltpu.SMEM)] + [pl.BlockSpec(memory_space=pltpu.VMEM)] * 16,
        out_specs=pl.BlockSpec(memory_space=pltpu.VMEM),
        compiler_params=pltpu.CompilerParams(vmem_limit_bytes=24 * 2**20),
        cost_estimate=pl.CostEstimate(flops=rows * 1024 * 4096 * 2, bytes_accessed=11 * 2**20, transcendentals=0),
        name="project",
    )(x, *blocks, *weights)


def local(queries, out_grad, keys, values, key_weight, value_weight, owner):
    q, g, k, v = queries[0], out_grad[0], keys[0], values[0]
    kw, vw = key_weight[0], value_weight[0]
    seq = lax.axis_index("seq")
    section = lax.axis_index("section")
    x = lax.div(seq, 4)
    h = lax.div(section, 4)
    y = lax.rem(section, 4)
    xs = x[None].astype(jnp.int32)

    def pair(matrix, d):
        at = lax.rem(x + d, 4) * PAIR
        return lax.dynamic_slice(matrix, (jnp.int32(0), at), (matrix.shape[0], PAIR))

    near = [jnp.concatenate([pair(m, d) for m in (q, g, k, v)], axis=0) for d in range(4)]
    far = [jnp.concatenate([pair(m, d) for m in (q, g)], axis=0) for d in range(4)]
    near = [near[0]] + [along_seq(near[d], dx=d) for d in (1, 2, 3)]
    far = [along_seq(far[d], dx=d, dz=1) for d in range(4)]
    mine = jnp.concatenate([b[:128] for b in near] + far, axis=0)
    other = along_seq(mine, dc=1)

    kw_z, vw_z = along_seq(kw, dz=1), along_seq(vw, dz=1)
    weights = [kw, vw, along_seq(kw, dc=1), along_seq(vw, dc=1)]
    weights += [kw_z, vw_z, along_seq(kw_z, dc=1), along_seq(vw_z, dc=1)]

    both = jnp.concatenate([mine, other], axis=0).reshape(16, 2, 64, PAIR)
    all_q = both[:, 0].reshape(1024, PAIR)
    all_g = both[:, 1].reshape(1024, PAIR)
    all_k = jnp.concatenate([b[128:256] for b in near], axis=0)
    all_v = jnp.concatenate([b[256:384] for b in near], axis=0)

    own = stats(all_q, all_g, all_k, all_v)
    parts = [own, along_seq(own, dc=1), along_seq(own, dz=1), along_seq(own, dz=1, dc=1)]

    size = 128 // CHUNKS
    sums = []
    for t in range(CHUNKS):
        k_t = all_k.reshape(4, 128, PAIR)[:, t * size:(t + 1) * size].reshape(4 * size, PAIR)
        v_t = all_v.reshape(4, 128, PAIR)[:, t * size:(t + 1) * size].reshape(4 * size, PAIR)
        a, b = grads(xs, parts, all_q, all_g, k_t, v_t)
        ra, rb, la, lb = along_seq(a, dx=1), along_seq(b, dx=1), along_seq(a, dx=3), along_seq(b, dx=3)
        oa, ob = along_seq(ra, dx=1), along_seq(lb, dx=3)
        part = project(xs, (a, b, ra, rb, oa, ob, la, lb), weights)
        part = part.reshape(4, size, 1024)

        def piece(d):
            return lax.dynamic_index_in_dim(part, lax.rem(y + d, 4), 0, keepdims=False)

        got = [piece(0)] + [along_section(piece(d), dy=d) for d in (1, 2, 3)]
        sums.append(sum(p.astype(F32) for p in got))
    total = jnp.stack(sums).astype(BF16)

    quarter = size // 4
    pieces = total.reshape(CHUNKS, 4, quarter, 1024)

    def slab(d):
        return lax.dynamic_index_in_dim(pieces, lax.rem(h + d, 4), 1, keepdims=False)

    got = [slab(0)] + [along_section(slab(d), dh=d) for d in (1, 2, 3)]
    total = sum(p.astype(F32) for p in got).astype(BF16).reshape(CHUNKS * quarter, 2, 2, 256)

    c = lax.rem(seq, 2)
    z = lax.rem(lax.div(seq, 2), 2)
    kept, sent = total[:, :, 0], total[:, :, 1]
    swapped = along_seq(sent, dc=1)
    by_core = jnp.where(c == 0, jnp.stack([kept, swapped]), jnp.stack([swapped, kept]))
    stay, leave = by_core[:, :, 0], by_core[:, :, 1]

    def both_moves(value, dh, dz):
        pairs = []
        for (s0, s1) in section_moves(dh, 0):
            for (q0, q1) in seq_moves(0, dz, 0):
                pairs.append((s0 * 16 + q0, s1 * 16 + q1))
        return lax.ppermute(value, ("section", "seq"), pairs)

    same = [stay] + [along_section(stay, dh=d) for d in (1, 2, 3)]
    cross = [both_moves(leave, d, 1) for d in range(4)]
    same, cross = jnp.stack(same), jnp.stack(cross)
    order = lax.rem(h - jnp.arange(4, dtype=jnp.int32) + 4, 4)
    same, cross = jnp.take(same, order, axis=0), jnp.take(cross, order, axis=0)
    rows = jnp.where(z == 0, jnp.stack([same, cross]), jnp.stack([cross, same]))
    rows = rows.reshape(2, 4, 2, CHUNKS, quarter, 256).transpose(0, 2, 3, 1, 4, 5).reshape(512, 256)

    spread = jnp.stack([rows] + [along_section(rows, dy=d) for d in (1, 2, 3)])
    spread = jnp.take(spread, lax.rem(y - jnp.arange(4, dtype=jnp.int32) + 4, 4), axis=0)
    result = spread.reshape(2048, 256)
    return jnp.where(section == owner[0], result, jnp.zeros((), BF16))[None]


def solution(mesh):
    in_specs = (P("section", "seq", None),) * 6 + (P(),)
    return jax.shard_map(local, mesh=mesh, in_specs=in_specs, out_specs=P("section", None, "seq"), check_vma=False)
```

```python
import functools

import jax
import jax.numpy as jnp
from jax import lax
from jax.experimental import pallas as pl
from jax.experimental.pallas import tpu as pltpu
from jax.sharding import PartitionSpec as P

HEAD = 256
PAIR = 512
SCALE = HEAD ** -0.5
F32 = jnp.float32
BF16 = jnp.bfloat16
NT = (((1,), (1,)), ((), ()))
NN = (((1,), (0,)), ((), ()))


def seq_moves(dx, dz, dc):
    pairs = []
    for x in range(4):
        for z in range(2):
            for c in range(2):
                pairs.append((x * 4 + z * 2 + c, ((x + dx) % 4) * 4 + ((z + dz) % 2) * 2 + (c + dc) % 2))
    return pairs


def section_moves(dh, dy):
    return [(h * 4 + y, ((h + dh) % 4) * 4 + (y + dy) % 4) for h in range(4) for y in range(4)]


def along_seq(value, dx=0, dz=0, dc=0):
    return lax.ppermute(value, "seq", seq_moves(dx, dz, dc))


def along_section(value, dh=0, dy=0):
    return lax.ppermute(value, "section", section_moves(dh, dy))


def along_both(value, dh, dz):
    pairs = [(s * 16 + i, t * 16 + j) for s, t in section_moves(dh, 0) for i, j in seq_moves(0, dz, 0)]
    return lax.ppermute(value, ("section", "seq"), pairs)


def dot(a, b, dims):
    return lax.dot_general(a, b, dims, preferred_element_type=F32)


def pack_kernel(q_ref, g_ref, k_ref, v_ref, out_ref):
    for to in range(8):
        cols = pl.ds(((to % 2) * 4 + to // 2) * HEAD, HEAD)
        out_ref[to, pl.ds(0, 64), :] = q_ref[:, cols]
        out_ref[to, pl.ds(64, 64), :] = g_ref[:, cols]
        out_ref[to, pl.ds(128, 128), :] = k_ref[:, cols]
        out_ref[to, pl.ds(256, 128), :] = v_ref[:, cols]


def pack(q, g, k, v):
    return pl.pallas_call(
        pack_kernel,
        out_shape=jax.ShapeDtypeStruct((8, 384, HEAD), BF16),
        in_specs=[pl.BlockSpec(memory_space=pltpu.VMEM)] * 4,
        out_specs=pl.BlockSpec(memory_space=pltpu.VMEM),
        compiler_params=pltpu.CompilerParams(vmem_limit_bytes=4 * 2**20),
        cost_estimate=pl.CostEstimate(flops=0, bytes_accessed=2**22, transcendentals=0),
        name="pack",
    )(q, g, k, v)


def query_quarter(mine, other, j, first):
    source = mine if j < 2 else other
    return jnp.concatenate([source[(j % 2) * 4 + i, pl.ds(first, 64), :] for i in range(4)], axis=0)


def key_rows(mine, first, blocks):
    return jnp.concatenate([mine[i, pl.ds(first, 128), :] for i in blocks], axis=0)


def stats_kernel(m_ref, o_ref, out_ref):
    out_ref[...] = jnp.zeros_like(out_ref)
    k, v = key_rows(m_ref, 128, range(8)), key_rows(m_ref, 256, range(8))
    for j in range(4):
        spot = pl.ds(j * 256, 256)
        s = dot(k, query_quarter(m_ref, o_ref, j, 0), NT) * SCALE
        gp = dot(v, query_quarter(m_ref, o_ref, j, 64), NT)
        peak = jnp.max(s, axis=0, keepdims=True)
        p = jnp.exp(s - peak)
        out_ref[pl.ds(0, 1), spot] = peak
        out_ref[pl.ds(1, 1), spot] = jnp.sum(p, axis=0, keepdims=True)
        out_ref[pl.ds(2, 1), spot] = jnp.sum(p * gp, axis=0, keepdims=True)


def stats(mine, other):
    return pl.pallas_call(
        stats_kernel,
        out_shape=jax.ShapeDtypeStruct((8, 1024), F32),
        in_specs=[pl.BlockSpec(memory_space=pltpu.VMEM)] * 2,
        out_specs=pl.BlockSpec(memory_space=pltpu.VMEM),
        compiler_params=pltpu.CompilerParams(vmem_limit_bytes=8 * 2**20),
        cost_estimate=pl.CostEstimate(flops=10**9, bytes_accessed=2**22, transcendentals=2**20),
        name="stats",
    )(mine, other)


def grads_kernel(half, s0, s1, m_ref, o_ref, out, p_s, d_s, q_s, g_s):
    for j in range(4):
        q_s[pl.ds(j * 256, 256), :] = query_quarter(m_ref, o_ref, j, 0)
        g_s[pl.ds(j * 256, 256), :] = query_quarter(m_ref, o_ref, j, 64)
    blocks = range(half * 4, half * 4 + 4)
    k, v = key_rows(m_ref, 128, blocks), key_rows(m_ref, 256, blocks)
    for j in range(4):
        rows = pl.ds(j * 256, 256)
        there = pl.ds((j ^ 2) * 256, 256)
        own, far = s0[pl.ds(0, 1), rows], s1[pl.ds(0, 1), there]
        peak = jnp.maximum(own, far)
        own, far = jnp.exp(own - peak), jnp.exp(far - peak)
        total = s0[pl.ds(1, 1), rows] * own + s1[pl.ds(1, 1), there] * far
        weighted = s0[pl.ds(2, 1), rows] * own + s1[pl.ds(2, 1), there] * far
        lse = peak + jnp.log(total)
        delta = weighted / total
        s = dot(k, q_s[rows, :], NT) * SCALE
        gp = dot(v, g_s[rows, :], NT)
        p = jnp.exp(s - lse)
        p_s[:, rows] = p.astype(BF16)
        d_s[:, rows] = (p * (gp - delta)).astype(BF16)
    out[:, pl.ds(0, HEAD)] = (dot(d_s[...], q_s[...], NN) * SCALE).astype(BF16)
    out[:, pl.ds(HEAD, HEAD)] = dot(p_s[...], g_s[...], NN).astype(BF16)


def grads(half, parts, mine, other):
    return pl.pallas_call(
        functools.partial(grads_kernel, half),
        out_shape=jax.ShapeDtypeStruct((512, 2 * HEAD), BF16),
        in_specs=[pl.BlockSpec(memory_space=pltpu.VMEM)] * 4,
        out_specs=pl.BlockSpec(memory_space=pltpu.VMEM),
        scratch_shapes=[pltpu.VMEM((512, 1024), BF16)] * 2 + [pltpu.VMEM((1024, HEAD), BF16)] * 2,
        compiler_params=pltpu.CompilerParams(vmem_limit_bytes=8 * 2**20),
        cost_estimate=pl.CostEstimate(flops=10**9, bytes_accessed=2**22, transcendentals=2**19),
        name="grads",
    )(*parts, mine, other)


def project_kernel(pos_ref, *refs):
    blocks, weights, outs, total = refs[:4], refs[4:8], refs[8:12], refs[12]
    x, y = pos_ref[0], pos_ref[1]
    for w, weight in enumerate(weights):
        acc = None
        for d, block in enumerate(blocks):
            cols = pl.ds(pl.multiple_of(lax.rem(x - d + 4, 4) * HEAD, HEAD), HEAD)
            for kind in range(2):
                term = dot(block[:, pl.ds(kind * HEAD, HEAD)], weight[pl.ds(kind * 256, 256), cols], NT)
                acc = term if acc is None else acc + term
        total[:, pl.ds(w * 256, 256)] = acc.astype(BF16)
    for d, out in enumerate(outs):
        out[...] = total[pl.ds(pl.multiple_of(lax.rem(y + d, 4) * 128, 128), 128), :]


def project(pos, blocks, weights):
    return pl.pallas_call(
        project_kernel,
        out_shape=(jax.ShapeDtypeStruct((128, 1024), BF16),) * 4,
        in_specs=[pl.BlockSpec(memory_space=pltpu.SMEM)] + [pl.BlockSpec(memory_space=pltpu.VMEM)] * 8,
        out_specs=(pl.BlockSpec(memory_space=pltpu.VMEM),) * 4,
        scratch_shapes=[pltpu.VMEM((512, 1024), BF16)],
        compiler_params=pltpu.CompilerParams(vmem_limit_bytes=8 * 2**20),
        cost_estimate=pl.CostEstimate(flops=512 * 1024 * 2048 * 2, bytes_accessed=7 * 2**20, transcendentals=0),
        name="project",
    )(pos, *blocks, *weights)


def sum_y_kernel(a, b, c, d, stay, leave):
    total = ((a[...].astype(F32) + b[...].astype(F32)) + (c[...].astype(F32) + d[...].astype(F32))).astype(BF16)
    stay[...] = total[:, :512]
    leave[...] = total[:, 512:]


def sum_y(terms):
    return pl.pallas_call(
        sum_y_kernel,
        out_shape=(jax.ShapeDtypeStruct((128, 512), BF16),) * 2,
        in_specs=[pl.BlockSpec(memory_space=pltpu.VMEM)] * 4,
        out_specs=(pl.BlockSpec(memory_space=pltpu.VMEM),) * 2,
        compiler_params=pltpu.CompilerParams(vmem_limit_bytes=4 * 2**20),
        cost_estimate=pl.CostEstimate(flops=2**20, bytes_accessed=5 * 2**19, transcendentals=0),
        name="sum_y",
    )(*terms)


def sum_pair_kernel(pos_ref, a, b, c, d, *refs):
    outs, total = refs[:4], refs[4]
    h = pos_ref[5]
    total[pl.ds(0, 128), :] = (a[...].astype(F32) + b[...].astype(F32)).astype(BF16)
    total[pl.ds(128, 128), :] = (c[...].astype(F32) + d[...].astype(F32)).astype(BF16)
    for d, out in enumerate(outs):
        out[...] = total[pl.ds(pl.multiple_of(lax.rem(h + d, 4) * 64, 64), 64), :]


def sum_pair(pos, terms):
    return pl.pallas_call(
        sum_pair_kernel,
        out_shape=(jax.ShapeDtypeStruct((64, 512), BF16),) * 4,
        in_specs=[pl.BlockSpec(memory_space=pltpu.SMEM)] + [pl.BlockSpec(memory_space=pltpu.VMEM)] * 4,
        out_specs=(pl.BlockSpec(memory_space=pltpu.VMEM),) * 4,
        scratch_shapes=[pltpu.VMEM((256, 512), BF16)],
        compiler_params=pltpu.CompilerParams(vmem_limit_bytes=2 * 2**20),
        cost_estimate=pl.CostEstimate(flops=2**18, bytes_accessed=2**19, transcendentals=0),
        name="sum_pair",
    )(pos, *terms)


def sum_z_kernel(a, b, c, d, *outs):
    total = ((a[...].astype(F32) + b[...].astype(F32)) + (c[...].astype(F32) + d[...].astype(F32))).astype(BF16)
    for i, out in enumerate(outs):
        out[...] = total[:, i * 256:(i + 1) * 256]


def sum_z(terms):
    return pl.pallas_call(
        sum_z_kernel,
        out_shape=(jax.ShapeDtypeStruct((64, 256), BF16),) * 2,
        in_specs=[pl.BlockSpec(memory_space=pltpu.VMEM)] * 4,
        out_specs=(pl.BlockSpec(memory_space=pltpu.VMEM),) * 2,
        compiler_params=pltpu.CompilerParams(vmem_limit_bytes=2 * 2**20),
        cost_estimate=pl.CostEstimate(flops=2**17, bytes_accessed=2**18, transcendentals=0),
        name="sum_z",
    )(*terms)


def place_kernel(pos_ref, g0, g1, g2, g3, out_ref):
    y, c, mine, h = pos_ref[1], pos_ref[3], pos_ref[4], pos_ref[5]
    for d, got in enumerate((g0, g1, g2, g3)):
        for e in range(4):
            piece = lax.rem(h - e + 4, 4)
            for i in range(2):
                from_y = lax.rem(y - d + 4, 4)
                at = (lax.div(piece, 2) * 2 + lax.div(from_y, 2)) * 512 + lax.rem(from_y, 2) * 256
                at += lax.rem(c + i, 2) * 128 + lax.rem(piece, 2) * 64
                value = got[e, :, pl.ds(i * 256, 256)]
                out_ref[pl.ds(pl.multiple_of(at, 64), 64), :] = jnp.where(mine == 1, value, jnp.zeros_like(value))


def place(pos, got):
    return pl.pallas_call(
        place_kernel,
        out_shape=jax.ShapeDtypeStruct((2048, 256), BF16),
        in_specs=[pl.BlockSpec(memory_space=pltpu.SMEM)] + [pl.BlockSpec(memory_space=pltpu.VMEM)] * 4,
        out_specs=pl.BlockSpec(memory_space=pltpu.VMEM),
        compiler_params=pltpu.CompilerParams(vmem_limit_bytes=2 * 2**20),
        cost_estimate=pl.CostEstimate(flops=0, bytes_accessed=2**21, transcendentals=0),
        name="place",
    )(pos, *got)


def local(queries, out_grad, keys, values, key_weight, value_weight, owner):
    q, g, k, v = queries[0], out_grad[0], keys[0], values[0]
    kw, vw = key_weight[0], value_weight[0]
    seq = lax.axis_index("seq")
    section = lax.axis_index("section")
    x = lax.div(seq, 4)
    h = lax.div(section, 4)
    y = lax.rem(section, 4)
    c = lax.rem(seq, 2)
    z = lax.rem(lax.div(seq, 2), 2)
    pos = jnp.stack([x, y, z, c, (section == owner[0]).astype(jnp.int32), h]).astype(jnp.int32)

    tie = lax.optimization_barrier
    rows = pack(q, g, k, v)
    groups = [[xx * 4 + zz * 2 + cc for xx in range(4) for zz in range(2)] for cc in range(2)]
    mine = lax.all_to_all(rows, "seq", 0, 0, axis_index_groups=groups)
    mine, kw, vw = tie((mine, kw, vw))
    other = along_seq(mine[:, :128], dc=1)

    def half(matrix, at):
        return lax.dynamic_slice(matrix, (jnp.int32(0), at * 1024), (256, 1024))

    weight = jnp.concatenate([half(kw, z), half(vw, z)], axis=0)
    weight_z = along_seq(jnp.concatenate([half(kw, 1 - z), half(vw, 1 - z)], axis=0), dz=1)
    weight_c = along_seq(weight, dc=1)

    own = stats(mine, other)
    parts = [own, along_seq(own, dc=1)]

    low, high = grads(0, parts, mine, other), grads(1, parts, mine, other)
    low_r, low_l = along_seq(low, dx=1), along_seq(low, dx=3)
    low_r, low_l, high = tie((low_r, low_l, high))
    low_o, high_l = along_seq(low_r, dx=1), along_seq(high, dx=3)
    low_o, high_l, weight_z = tie((low_o, high_l, weight_z))
    high_r, high_o = along_seq(high, dx=1), along_seq(high_l, dx=3)
    weights = (weight, weight_c, weight_z, along_seq(weight_z, dc=1))

    def sum_two(pieces):
        stay, leave = sum_y([pieces[0]] + [along_section(pieces[d], dy=d) for d in (1, 2, 3)])
        return [stay, along_seq(leave, dz=1)]

    low_pieces = project(pos, (low, low_r, low_o, low_l), weights)
    high_r, high_o, first = tie((high_r, high_o, low_pieces[0]))
    high_pieces = project(pos, (high, high_r, high_o, high_l), weights)
    terms = sum_two([first, *low_pieces[1:]]) + sum_two(high_pieces)

    pieces = sum_pair(pos, terms)
    cols = sum_z([pieces[0]] + [along_section(pieces[d], dh=d) for d in (1, 2, 3)])

    rows = jnp.concatenate([cols[0], along_seq(cols[1], dc=1)], axis=1)
    rows = jnp.stack([rows] + [along_section(rows, dh=d) for d in (1, 2, 3)])
    return place(pos, [rows] + [along_section(rows, dy=d) for d in (1, 2, 3)])[None]


def solution(mesh):
    in_specs = (P("section", "seq", None),) * 6 + (P(),)
    return jax.shard_map(local, mesh=mesh, in_specs=in_specs, out_specs=P("section", None, "seq"), check_vma=False)
```

```python
import functools

import jax
import jax.numpy as jnp
from jax import lax
from jax.experimental import pallas as pl
from jax.experimental.pallas import tpu as pltpu
from jax.sharding import PartitionSpec as P

HEAD = 256
PAIR = 512
SCALE = HEAD ** -0.5
F32 = jnp.float32
BF16 = jnp.bfloat16
NT = (((1,), (1,)), ((), ()))
NN = (((1,), (0,)), ((), ()))


def seq_moves(dx, dz, dc):
    pairs = []
    for x in range(4):
        for z in range(2):
            for c in range(2):
                pairs.append((x * 4 + z * 2 + c, ((x + dx) % 4) * 4 + ((z + dz) % 2) * 2 + (c + dc) % 2))
    return pairs


def section_moves(dh, dy):
    return [(h * 4 + y, ((h + dh) % 4) * 4 + (y + dy) % 4) for h in range(4) for y in range(4)]


def along_seq(value, dx=0, dz=0, dc=0):
    return lax.ppermute(value, "seq", seq_moves(dx, dz, dc))


def along_section(value, dh=0, dy=0):
    return lax.ppermute(value, "section", section_moves(dh, dy))


def along_both(value, dh, dz):
    pairs = [(s * 16 + i, t * 16 + j) for s, t in section_moves(dh, 0) for i, j in seq_moves(0, dz, 0)]
    return lax.ppermute(value, ("section", "seq"), pairs)


def dot(a, b, dims):
    return lax.dot_general(a, b, dims, preferred_element_type=F32)


def pack_kernel(q_ref, g_ref, k_ref, v_ref, out_ref):
    for to in range(8):
        cols = pl.ds(((to % 2) * 4 + to // 2) * HEAD, HEAD)
        out_ref[to, pl.ds(0, 64), :] = q_ref[:, cols]
        out_ref[to, pl.ds(64, 64), :] = g_ref[:, cols]
        out_ref[to, pl.ds(128, 128), :] = k_ref[:, cols]
        out_ref[to, pl.ds(256, 128), :] = v_ref[:, cols]


def pack(q, g, k, v):
    return pl.pallas_call(
        pack_kernel,
        out_shape=jax.ShapeDtypeStruct((8, 384, HEAD), BF16),
        in_specs=[pl.BlockSpec(memory_space=pltpu.VMEM)] * 4,
        out_specs=pl.BlockSpec(memory_space=pltpu.VMEM),
        compiler_params=pltpu.CompilerParams(vmem_limit_bytes=4 * 2**20),
        cost_estimate=pl.CostEstimate(flops=0, bytes_accessed=2**22, transcendentals=0),
        name="pack",
    )(q, g, k, v)


def query_quarter(mine, other, j, first):
    source = mine if j < 2 else other
    return jnp.concatenate([source[(j % 2) * 4 + i, pl.ds(first, 64), :] for i in range(4)], axis=0)


def key_rows(mine, first, blocks):
    return jnp.concatenate([mine[i, pl.ds(first, 128), :] for i in blocks], axis=0)


def stats_kernel(m_ref, o_ref, out_ref):
    out_ref[...] = jnp.zeros_like(out_ref)
    k, v = key_rows(m_ref, 128, range(8)), key_rows(m_ref, 256, range(8))
    for j in range(4):
        spot = pl.ds(j * 256, 256)
        s = dot(k, query_quarter(m_ref, o_ref, j, 0), NT) * SCALE
        gp = dot(v, query_quarter(m_ref, o_ref, j, 64), NT)
        peak = jnp.max(s, axis=0, keepdims=True)
        p = jnp.exp(s - peak)
        out_ref[pl.ds(0, 1), spot] = peak
        out_ref[pl.ds(1, 1), spot] = jnp.sum(p, axis=0, keepdims=True)
        out_ref[pl.ds(2, 1), spot] = jnp.sum(p * gp, axis=0, keepdims=True)


def stats(mine, other):
    return pl.pallas_call(
        stats_kernel,
        out_shape=jax.ShapeDtypeStruct((8, 1024), F32),
        in_specs=[pl.BlockSpec(memory_space=pltpu.VMEM)] * 2,
        out_specs=pl.BlockSpec(memory_space=pltpu.VMEM),
        compiler_params=pltpu.CompilerParams(vmem_limit_bytes=8 * 2**20),
        cost_estimate=pl.CostEstimate(flops=10**9, bytes_accessed=2**22, transcendentals=2**20),
        name="stats",
    )(mine, other)


def grads_kernel(half, s0, s1, m_ref, o_ref, out, p_s, d_s, q_s, g_s):
    for j in range(4):
        q_s[pl.ds(j * 256, 256), :] = query_quarter(m_ref, o_ref, j, 0)
        g_s[pl.ds(j * 256, 256), :] = query_quarter(m_ref, o_ref, j, 64)
    blocks = range(half * 4, half * 4 + 4)
    k, v = key_rows(m_ref, 128, blocks), key_rows(m_ref, 256, blocks)
    for j in range(4):
        rows = pl.ds(j * 256, 256)
        there = pl.ds((j ^ 2) * 256, 256)
        own, far = s0[pl.ds(0, 1), rows], s1[pl.ds(0, 1), there]
        peak = jnp.maximum(own, far)
        own, far = jnp.exp(own - peak), jnp.exp(far - peak)
        total = s0[pl.ds(1, 1), rows] * own + s1[pl.ds(1, 1), there] * far
        weighted = s0[pl.ds(2, 1), rows] * own + s1[pl.ds(2, 1), there] * far
        lse = peak + jnp.log(total)
        delta = weighted / total
        s = dot(k, q_s[rows, :], NT) * SCALE
        gp = dot(v, g_s[rows, :], NT)
        p = jnp.exp(s - lse)
        p_s[:, rows] = p.astype(BF16)
        d_s[:, rows] = (p * (gp - delta)).astype(BF16)
    out[:, pl.ds(0, HEAD)] = (dot(d_s[...], q_s[...], NN) * SCALE).astype(BF16)
    out[:, pl.ds(HEAD, HEAD)] = dot(p_s[...], g_s[...], NN).astype(BF16)


def grads(half, parts, mine, other):
    return pl.pallas_call(
        functools.partial(grads_kernel, half),
        out_shape=jax.ShapeDtypeStruct((512, 2 * HEAD), BF16),
        in_specs=[pl.BlockSpec(memory_space=pltpu.VMEM)] * 4,
        out_specs=pl.BlockSpec(memory_space=pltpu.VMEM),
        scratch_shapes=[pltpu.VMEM((512, 1024), BF16)] * 2 + [pltpu.VMEM((1024, HEAD), BF16)] * 2,
        compiler_params=pltpu.CompilerParams(vmem_limit_bytes=8 * 2**20),
        cost_estimate=pl.CostEstimate(flops=10**9, bytes_accessed=2**22, transcendentals=2**19),
        name="grads",
    )(*parts, mine, other)


def head_cols(x, d):
    return pl.ds(pl.multiple_of(lax.rem(x - d + 4, 4) * HEAD, HEAD), HEAD)


def project_kernel(pos_ref, *refs):
    blocks, weights, out = refs[:6], refs[6:8], refs[8]
    for half in range(2):
        for w, weight in enumerate(weights):
            acc = None
            for n, d in enumerate((0, 1, 3)):
                for kind in range(2):
                    block = blocks[2 * n + half][:, pl.ds(kind * HEAD, HEAD)]
                    term = dot(block, weight[pl.ds(kind * 256, 256), head_cols(pos_ref[0], d)], NT)
                    acc = term if acc is None else acc + term
            out[pl.ds(half * 512, 512), pl.ds(w * 256, 256)] = acc.astype(out.dtype)


def project(pos, blocks, weights):
    return pl.pallas_call(
        project_kernel,
        out_shape=jax.ShapeDtypeStruct((1024, 512), BF16),
        in_specs=[pl.BlockSpec(memory_space=pltpu.SMEM)] + [pl.BlockSpec(memory_space=pltpu.VMEM)] * 8,
        out_specs=pl.BlockSpec(memory_space=pltpu.VMEM),
        compiler_params=pltpu.CompilerParams(vmem_limit_bytes=8 * 2**20),
        cost_estimate=pl.CostEstimate(flops=1024 * 512 * 1536 * 2, bytes_accessed=6 * 2**20, transcendentals=0),
        name="project",
    )(pos, *blocks, *weights)


def finish_kernel(pos_ref, part, low, high, w0, w1, *refs):
    outs, total = refs[:4], refs[4]
    x, y = pos_ref[0], pos_ref[1]
    for half, block in enumerate((low, high)):
        for w, weight in enumerate((w0, w1)):
            spot = (pl.ds(half * 512, 512), pl.ds(w * 256, 256))
            acc = part[spot].astype(F32)
            for kind in range(2):
                acc = acc + dot(block[:, pl.ds(kind * HEAD, HEAD)], weight[pl.ds(kind * 256, 256), head_cols(x, 2)], NT)
            total[spot] = acc.astype(BF16)
    for d, out in enumerate(outs):
        out[...] = total[pl.ds(pl.multiple_of(lax.rem(y + d, 4) * 256, 256), 256), :]


def finish(pos, part, low, high, weights):
    return pl.pallas_call(
        finish_kernel,
        out_shape=(jax.ShapeDtypeStruct((256, 512), BF16),) * 4,
        in_specs=[pl.BlockSpec(memory_space=pltpu.SMEM)] + [pl.BlockSpec(memory_space=pltpu.VMEM)] * 5,
        out_specs=(pl.BlockSpec(memory_space=pltpu.VMEM),) * 4,
        scratch_shapes=[pltpu.VMEM((1024, 512), BF16)],
        compiler_params=pltpu.CompilerParams(vmem_limit_bytes=8 * 2**20),
        cost_estimate=pl.CostEstimate(flops=1024 * 512 * 512 * 2, bytes_accessed=5 * 2**20, transcendentals=0),
        name="finish",
    )(pos, part, low, high, *weights)


def sum_y_kernel(a, b, c, d, out):
    out[...] = ((a[...].astype(F32) + b[...].astype(F32)) + (c[...].astype(F32) + d[...].astype(F32))).astype(BF16)


def sum_y(terms):
    return pl.pallas_call(
        sum_y_kernel,
        out_shape=jax.ShapeDtypeStruct((256, 512), BF16),
        in_specs=[pl.BlockSpec(memory_space=pltpu.VMEM)] * 4,
        out_specs=pl.BlockSpec(memory_space=pltpu.VMEM),
        compiler_params=pltpu.CompilerParams(vmem_limit_bytes=4 * 2**20),
        cost_estimate=pl.CostEstimate(flops=2**19, bytes_accessed=5 * 2**18, transcendentals=0),
        name="sum_y",
    )(*terms)


def sum_pair_kernel(pos_ref, *refs):
    terms, outs, total = refs[:5], refs[5:9], refs[9]
    h = pos_ref[5]
    acc = terms[0][...].astype(F32)
    for term in terms[1:]:
        acc = acc + term[...].astype(F32)
    total[...] = acc.astype(BF16)
    for d, out in enumerate(outs):
        out[...] = total[pl.ds(pl.multiple_of(lax.rem(h + d, 4) * 64, 64), 64), :]


def sum_pair(pos, terms):
    return pl.pallas_call(
        sum_pair_kernel,
        out_shape=(jax.ShapeDtypeStruct((64, 512), BF16),) * 4,
        in_specs=[pl.BlockSpec(memory_space=pltpu.SMEM)] + [pl.BlockSpec(memory_space=pltpu.VMEM)] * 5,
        out_specs=(pl.BlockSpec(memory_space=pltpu.VMEM),) * 4,
        scratch_shapes=[pltpu.VMEM((256, 512), BF16)],
        compiler_params=pltpu.CompilerParams(vmem_limit_bytes=4 * 2**20),
        cost_estimate=pl.CostEstimate(flops=2**19, bytes_accessed=5 * 2**18, transcendentals=0),
        name="sum_pair",
    )(pos, *terms)


def sum_z_kernel(a, b, c, d, *outs):
    total = ((a[...].astype(F32) + b[...].astype(F32)) + (c[...].astype(F32) + d[...].astype(F32))).astype(BF16)
    for i, out in enumerate(outs):
        out[...] = total[:, i * 256:(i + 1) * 256]


def sum_z(terms):
    return pl.pallas_call(
        sum_z_kernel,
        out_shape=(jax.ShapeDtypeStruct((64, 256), BF16),) * 2,
        in_specs=[pl.BlockSpec(memory_space=pltpu.VMEM)] * 4,
        out_specs=(pl.BlockSpec(memory_space=pltpu.VMEM),) * 2,
        compiler_params=pltpu.CompilerParams(vmem_limit_bytes=2 * 2**20),
        cost_estimate=pl.CostEstimate(flops=2**17, bytes_accessed=2**18, transcendentals=0),
        name="sum_z",
    )(*terms)


def place_kernel(pos_ref, g0, g1, g2, g3, out_ref):
    y, c, mine, h = pos_ref[1], pos_ref[3], pos_ref[4], pos_ref[5]
    for d, got in enumerate((g0, g1, g2, g3)):
        for e in range(4):
            piece = lax.rem(h - e + 4, 4)
            for i in range(2):
                at = lax.rem(y - d + 4, 4) * 512 + lax.div(piece, 2) * 256 + lax.rem(c + i, 2) * 128 + lax.rem(piece, 2) * 64
                value = got[e, :, pl.ds(i * 256, 256)]
                out_ref[pl.ds(pl.multiple_of(at, 64), 64), :] = jnp.where(mine == 1, value, jnp.zeros_like(value))


def place(pos, got):
    return pl.pallas_call(
        place_kernel,
        out_shape=jax.ShapeDtypeStruct((2048, 256), BF16),
        in_specs=[pl.BlockSpec(memory_space=pltpu.SMEM)] + [pl.BlockSpec(memory_space=pltpu.VMEM)] * 4,
        out_specs=pl.BlockSpec(memory_space=pltpu.VMEM),
        compiler_params=pltpu.CompilerParams(vmem_limit_bytes=2 * 2**20),
        cost_estimate=pl.CostEstimate(flops=0, bytes_accessed=2**21, transcendentals=0),
        name="place",
    )(pos, *got)


def local(queries, out_grad, keys, values, key_weight, value_weight, owner):
    q, g, k, v = queries[0], out_grad[0], keys[0], values[0]
    kw, vw = key_weight[0], value_weight[0]
    seq = lax.axis_index("seq")
    section = lax.axis_index("section")
    x = lax.div(seq, 4)
    h = lax.div(section, 4)
    y = lax.rem(section, 4)
    c = lax.rem(seq, 2)
    z = lax.rem(lax.div(seq, 2), 2)
    pos = jnp.stack([x, y, z, c, (section == owner[0]).astype(jnp.int32), h]).astype(jnp.int32)

    tie = lax.optimization_barrier
    rows = pack(q, g, k, v)
    groups = [[xx * 4 + zz * 2 + cc for xx in range(4) for zz in range(2)] for cc in range(2)]
    mine = lax.all_to_all(rows, "seq", 0, 0, axis_index_groups=groups)
    mine, kw, vw = tie((mine, kw, vw))
    other = along_seq(mine[:, :128], dc=1)

    def half(matrix, at):
        return lax.dynamic_slice(matrix, (jnp.int32(0), at * 1024), (256, 1024))

    weight = jnp.concatenate([half(kw, z), half(vw, z)], axis=0)
    weight_z = along_seq(jnp.concatenate([half(kw, 1 - z), half(vw, 1 - z)], axis=0), dz=1)
    weight_c = along_seq(weight, dc=1)

    own = stats(mine, other)
    parts = [own, along_seq(own, dc=1)]

    low, high = grads(0, parts, mine, other), grads(1, parts, mine, other)
    low_r, low_l = along_seq(low, dx=1), along_seq(low, dx=3)
    high_r, high_l = along_seq(high, dx=1), along_seq(high, dx=3)
    low_r, low_l, high_r, high_l, weight_z = tie((low_r, low_l, high_r, high_l, weight_z))
    low_o, high_o = along_seq(low_r, dx=1), along_seq(high_l, dx=3)
    weight_zc = along_seq(weight_z, dc=1)
    blocks = (low, high, low_r, high_r, low_l, high_l)
    stay, leave = project(pos, blocks, (weight, weight_c)), project(pos, blocks, (weight_z, weight_zc))

    def to_y(pieces):
        return [pieces[0]] + [along_section(pieces[d], dy=d) for d in (1, 2, 3)]

    leave = sum_y(to_y(finish(pos, leave, low_o, high_o, (weight_z, weight_zc))))
    terms = to_y(finish(pos, stay, low_o, high_o, (weight, weight_c))) + [along_seq(leave, dz=1)]

    pieces = sum_pair(pos, terms)
    cols = sum_z([pieces[0]] + [along_section(pieces[d], dh=d) for d in (1, 2, 3)])

    rows = jnp.concatenate([cols[0], along_seq(cols[1], dc=1)], axis=1)
    rows = jnp.stack([rows] + [along_section(rows, dh=d) for d in (1, 2, 3)])
    return place(pos, [rows] + [along_section(rows, dy=d) for d in (1, 2, 3)])[None]


def solution(mesh):
    in_specs = (P("section", "seq", None),) * 6 + (P(),)
    return jax.shard_map(local, mesh=mesh, in_specs=in_specs, out_specs=P("section", None, "seq"), check_vma=False)
```

```python
import functools

import jax
import jax.numpy as jnp
from jax import lax
from jax.experimental import pallas as pl
from jax.experimental.pallas import tpu as pltpu
from jax.sharding import PartitionSpec as P

HEAD = 256
PAIR = 512
SCALE = HEAD ** -0.5
F32 = jnp.float32
BF16 = jnp.bfloat16
NT = (((1,), (1,)), ((), ()))
NN = (((1,), (0,)), ((), ()))


def seq_moves(dx, dz, dc):
    pairs = []
    for x in range(4):
        for z in range(2):
            for c in range(2):
                pairs.append((x * 4 + z * 2 + c, ((x + dx) % 4) * 4 + ((z + dz) % 2) * 2 + (c + dc) % 2))
    return pairs


def section_moves(dh, dy):
    return [(h * 4 + y, ((h + dh) % 4) * 4 + (y + dy) % 4) for h in range(4) for y in range(4)]


def along_seq(value, dx=0, dz=0, dc=0):
    return lax.ppermute(value, "seq", seq_moves(dx, dz, dc))


def along_section(value, dh=0, dy=0):
    return lax.ppermute(value, "section", section_moves(dh, dy))


def along_both(value, dh, dz):
    pairs = [(s * 16 + i, t * 16 + j) for s, t in section_moves(dh, 0) for i, j in seq_moves(0, dz, 0)]
    return lax.ppermute(value, ("section", "seq"), pairs)


def dot(a, b, dims):
    return lax.dot_general(a, b, dims, preferred_element_type=F32)


def pack_kernel(rows_ref, out_ref):
    for to in range(8):
        out_ref[to] = rows_ref[:, pl.ds(((to % 2) * 4 + to // 2) * HEAD, HEAD)]


def pack(rows):
    return pl.pallas_call(
        pack_kernel,
        out_shape=jax.ShapeDtypeStruct((8, 384, HEAD), BF16),
        in_specs=[pl.BlockSpec(memory_space=pltpu.VMEM)],
        out_specs=pl.BlockSpec(memory_space=pltpu.VMEM),
        compiler_params=pltpu.CompilerParams(vmem_limit_bytes=4 * 2**20),
        cost_estimate=pl.CostEstimate(flops=0, bytes_accessed=2**22, transcendentals=0),
        name="pack",
    )(rows)


def query_quarter(mine, other, j, first):
    source = mine if j < 2 else other
    return jnp.concatenate([source[(j % 2) * 4 + i, pl.ds(first, 64), :] for i in range(4)], axis=0)


def key_rows(mine, first, blocks):
    return jnp.concatenate([mine[i, pl.ds(first, 128), :] for i in blocks], axis=0)


def stats_kernel(m_ref, o_ref, out_ref):
    out_ref[...] = jnp.zeros_like(out_ref)
    k, v = key_rows(m_ref, 128, range(8)), key_rows(m_ref, 256, range(8))
    for j in range(4):
        spot = pl.ds(j * 256, 256)
        s = dot(k, query_quarter(m_ref, o_ref, j, 0), NT) * SCALE
        gp = dot(v, query_quarter(m_ref, o_ref, j, 64), NT)
        peak = jnp.max(s, axis=0, keepdims=True)
        p = jnp.exp(s - peak)
        out_ref[pl.ds(0, 1), spot] = peak
        out_ref[pl.ds(1, 1), spot] = jnp.sum(p, axis=0, keepdims=True)
        out_ref[pl.ds(2, 1), spot] = jnp.sum(p * gp, axis=0, keepdims=True)


def stats(mine, other):
    return pl.pallas_call(
        stats_kernel,
        out_shape=jax.ShapeDtypeStruct((8, 1024), F32),
        in_specs=[pl.BlockSpec(memory_space=pltpu.VMEM)] * 2,
        out_specs=pl.BlockSpec(memory_space=pltpu.VMEM),
        compiler_params=pltpu.CompilerParams(vmem_limit_bytes=8 * 2**20),
        cost_estimate=pl.CostEstimate(flops=10**9, bytes_accessed=2**22, transcendentals=2**20),
        name="stats",
    )(mine, other)


def grads_kernel(half, s0, s1, m_ref, o_ref, out, p_s, d_s, q_s, g_s):
    for j in range(4):
        q_s[pl.ds(j * 256, 256), :] = query_quarter(m_ref, o_ref, j, 0)
        g_s[pl.ds(j * 256, 256), :] = query_quarter(m_ref, o_ref, j, 64)
    blocks = range(half * 4, half * 4 + 4)
    k, v = key_rows(m_ref, 128, blocks), key_rows(m_ref, 256, blocks)
    for j in range(4):
        rows = pl.ds(j * 256, 256)
        there = pl.ds((j ^ 2) * 256, 256)
        own, far = s0[pl.ds(0, 1), rows], s1[pl.ds(0, 1), there]
        peak = jnp.maximum(own, far)
        own, far = jnp.exp(own - peak), jnp.exp(far - peak)
        total = s0[pl.ds(1, 1), rows] * own + s1[pl.ds(1, 1), there] * far
        weighted = s0[pl.ds(2, 1), rows] * own + s1[pl.ds(2, 1), there] * far
        lse = peak + jnp.log(total)
        delta = weighted / total
        s = dot(k, q_s[rows, :], NT) * SCALE
        gp = dot(v, g_s[rows, :], NT)
        p = jnp.exp(s - lse)
        p_s[:, rows] = p.astype(BF16)
        d_s[:, rows] = (p * (gp - delta)).astype(BF16)
    out[:, pl.ds(0, HEAD)] = (dot(d_s[...], q_s[...], NN) * SCALE).astype(BF16)
    out[:, pl.ds(HEAD, HEAD)] = dot(p_s[...], g_s[...], NN).astype(BF16)


def grads(half, parts, mine, other):
    return pl.pallas_call(
        functools.partial(grads_kernel, half),
        out_shape=jax.ShapeDtypeStruct((512, 2 * HEAD), BF16),
        in_specs=[pl.BlockSpec(memory_space=pltpu.VMEM)] * 4,
        out_specs=pl.BlockSpec(memory_space=pltpu.VMEM),
        scratch_shapes=[pltpu.VMEM((512, 1024), BF16)] * 2 + [pltpu.VMEM((1024, HEAD), BF16)] * 2,
        compiler_params=pltpu.CompilerParams(vmem_limit_bytes=8 * 2**20),
        cost_estimate=pl.CostEstimate(flops=10**9, bytes_accessed=2**22, transcendentals=2**19),
        name="grads",
    )(*parts, mine, other)


def head_cols(x, d):
    return pl.ds(pl.multiple_of(lax.rem(x - d + 4, 4) * HEAD, HEAD), HEAD)


def project_kernel(pos_ref, *refs):
    blocks, weights, out = refs[:6], refs[6:8], refs[8]
    for half in range(2):
        for w, weight in enumerate(weights):
            acc = None
            for n, d in enumerate((0, 1, 3)):
                for kind in range(2):
                    block = blocks[2 * n + half][:, pl.ds(kind * HEAD, HEAD)]
                    term = dot(block, weight[pl.ds(kind * 256, 256), head_cols(pos_ref[0], d)], NT)
                    acc = term if acc is None else acc + term
            out[pl.ds(half * 512, 512), pl.ds(w * 256, 256)] = acc.astype(out.dtype)


def project(pos, blocks, weights):
    return pl.pallas_call(
        project_kernel,
        out_shape=jax.ShapeDtypeStruct((1024, 512), BF16),
        in_specs=[pl.BlockSpec(memory_space=pltpu.SMEM)] + [pl.BlockSpec(memory_space=pltpu.VMEM)] * 8,
        out_specs=pl.BlockSpec(memory_space=pltpu.VMEM),
        compiler_params=pltpu.CompilerParams(vmem_limit_bytes=8 * 2**20),
        cost_estimate=pl.CostEstimate(flops=1024 * 512 * 1536 * 2, bytes_accessed=6 * 2**20, transcendentals=0),
        name="project",
    )(pos, *blocks, *weights)


def finish_kernel(pos_ref, part, low, high, w0, w1, *refs):
    outs, total = refs[:4], refs[4]
    x, y = pos_ref[0], pos_ref[1]
    for half, block in enumerate((low, high)):
        for w, weight in enumerate((w0, w1)):
            spot = (pl.ds(half * 512, 512), pl.ds(w * 256, 256))
            acc = part[spot].astype(F32)
            for kind in range(2):
                acc = acc + dot(block[:, pl.ds(kind * HEAD, HEAD)], weight[pl.ds(kind * 256, 256), head_cols(x, 2)], NT)
            total[spot] = acc.astype(BF16)
    for d, out in enumerate(outs):
        out[...] = total[pl.ds(pl.multiple_of(lax.rem(y + d, 4) * 256, 256), 256), :]


def finish(pos, part, low, high, weights):
    return pl.pallas_call(
        finish_kernel,
        out_shape=(jax.ShapeDtypeStruct((256, 512), BF16),) * 4,
        in_specs=[pl.BlockSpec(memory_space=pltpu.SMEM)] + [pl.BlockSpec(memory_space=pltpu.VMEM)] * 5,
        out_specs=(pl.BlockSpec(memory_space=pltpu.VMEM),) * 4,
        scratch_shapes=[pltpu.VMEM((1024, 512), BF16)],
        compiler_params=pltpu.CompilerParams(vmem_limit_bytes=8 * 2**20),
        cost_estimate=pl.CostEstimate(flops=1024 * 512 * 512 * 2, bytes_accessed=5 * 2**20, transcendentals=0),
        name="finish",
    )(pos, part, low, high, *weights)


def sum_y_kernel(a, b, c, d, out):
    out[...] = ((a[...].astype(F32) + b[...].astype(F32)) + (c[...].astype(F32) + d[...].astype(F32))).astype(BF16)


def sum_y(terms):
    return pl.pallas_call(
        sum_y_kernel,
        out_shape=jax.ShapeDtypeStruct((256, 512), BF16),
        in_specs=[pl.BlockSpec(memory_space=pltpu.VMEM)] * 4,
        out_specs=pl.BlockSpec(memory_space=pltpu.VMEM),
        compiler_params=pltpu.CompilerParams(vmem_limit_bytes=4 * 2**20),
        cost_estimate=pl.CostEstimate(flops=2**19, bytes_accessed=5 * 2**18, transcendentals=0),
        name="sum_y",
    )(*terms)


def sum_pair_kernel(pos_ref, *refs):
    terms, outs, total = refs[:5], refs[5:9], refs[9]
    h = pos_ref[5]
    acc = terms[0][...].astype(F32)
    for term in terms[1:]:
        acc = acc + term[...].astype(F32)
    total[...] = acc.astype(BF16)
    for d, out in enumerate(outs):
        out[...] = total[pl.ds(pl.multiple_of(lax.rem(h + d, 4) * 64, 64), 64), :]


def sum_pair(pos, terms):
    return pl.pallas_call(
        sum_pair_kernel,
        out_shape=(jax.ShapeDtypeStruct((64, 512), BF16),) * 4,
        in_specs=[pl.BlockSpec(memory_space=pltpu.SMEM)] + [pl.BlockSpec(memory_space=pltpu.VMEM)] * 5,
        out_specs=(pl.BlockSpec(memory_space=pltpu.VMEM),) * 4,
        scratch_shapes=[pltpu.VMEM((256, 512), BF16)],
        compiler_params=pltpu.CompilerParams(vmem_limit_bytes=4 * 2**20),
        cost_estimate=pl.CostEstimate(flops=2**19, bytes_accessed=5 * 2**18, transcendentals=0),
        name="sum_pair",
    )(pos, *terms)


def sum_z_kernel(a, b, c, d, *outs):
    total = ((a[...].astype(F32) + b[...].astype(F32)) + (c[...].astype(F32) + d[...].astype(F32))).astype(BF16)
    for i, out in enumerate(outs):
        out[...] = total[:, i * 256:(i + 1) * 256]


def sum_z(terms):
    return pl.pallas_call(
        sum_z_kernel,
        out_shape=(jax.ShapeDtypeStruct((64, 256), BF16),) * 2,
        in_specs=[pl.BlockSpec(memory_space=pltpu.VMEM)] * 4,
        out_specs=(pl.BlockSpec(memory_space=pltpu.VMEM),) * 2,
        compiler_params=pltpu.CompilerParams(vmem_limit_bytes=2 * 2**20),
        cost_estimate=pl.CostEstimate(flops=2**17, bytes_accessed=2**18, transcendentals=0),
        name="sum_z",
    )(*terms)


def place_kernel(pos_ref, g0, g1, g2, g3, out_ref):
    y, c, mine, h = pos_ref[1], pos_ref[3], pos_ref[4], pos_ref[5]
    for d, got in enumerate((g0, g1, g2, g3)):
        for e in range(4):
            piece = lax.rem(h - e + 4, 4)
            for i in range(2):
                at = lax.rem(y - d + 4, 4) * 512 + lax.div(piece, 2) * 256 + lax.rem(c + i, 2) * 128 + lax.rem(piece, 2) * 64
                value = got[e, :, pl.ds(i * 256, 256)]
                out_ref[pl.ds(pl.multiple_of(at, 64), 64), :] = jnp.where(mine == 1, value, jnp.zeros_like(value))


def place(pos, got):
    return pl.pallas_call(
        place_kernel,
        out_shape=jax.ShapeDtypeStruct((2048, 256), BF16),
        in_specs=[pl.BlockSpec(memory_space=pltpu.SMEM)] + [pl.BlockSpec(memory_space=pltpu.VMEM)] * 4,
        out_specs=pl.BlockSpec(memory_space=pltpu.VMEM),
        compiler_params=pltpu.CompilerParams(vmem_limit_bytes=2 * 2**20),
        cost_estimate=pl.CostEstimate(flops=0, bytes_accessed=2**21, transcendentals=0),
        name="place",
    )(pos, *got)


def local(queries, out_grad, keys, values, key_weight, value_weight, owner):
    q, g, k, v = queries[0], out_grad[0], keys[0], values[0]
    kw, vw = key_weight[0], value_weight[0]
    seq = lax.axis_index("seq")
    section = lax.axis_index("section")
    x = lax.div(seq, 4)
    h = lax.div(section, 4)
    y = lax.rem(section, 4)
    c = lax.rem(seq, 2)
    z = lax.rem(lax.div(seq, 2), 2)
    pos = jnp.stack([x, y, z, c, (section == owner[0]).astype(jnp.int32), h]).astype(jnp.int32)

    tie = lax.optimization_barrier
    rows = pack(jnp.concatenate([q, g, k, v], axis=0))
    groups = [[xx * 4 + zz * 2 + cc for xx in range(4) for zz in range(2)] for cc in range(2)]
    mine = lax.all_to_all(rows, "seq", 0, 0, axis_index_groups=groups)
    other = along_seq(mine[:, :128], dc=1)

    own = stats(mine, other)
    own, kw, vw = tie((own, kw, vw))
    parts = [own, along_seq(own, dc=1)]

    def half(matrix, at):
        return lax.dynamic_slice(matrix, (jnp.int32(0), at * 1024), (256, 1024))

    weight = jnp.concatenate([half(kw, z), half(vw, z)], axis=0)
    weight_z = along_seq(jnp.concatenate([half(kw, 1 - z), half(vw, 1 - z)], axis=0), dz=1)
    weight_c = along_seq(weight, dc=1)

    low, high = grads(0, parts, mine, other), grads(1, parts, mine, other)
    low_r, low_l = along_seq(low, dx=1), along_seq(low, dx=3)
    high_r, high_l = along_seq(high, dx=1), along_seq(high, dx=3)
    low_r, low_l, high_r, high_l, weight_z = tie((low_r, low_l, high_r, high_l, weight_z))
    low_o, high_o = along_seq(low_r, dx=1), along_seq(high_l, dx=3)
    weight_zc = along_seq(weight_z, dc=1)
    blocks = (low, high, low_r, high_r, low_l, high_l)
    stay, leave = project(pos, blocks, (weight, weight_c)), project(pos, blocks, (weight_z, weight_zc))

    def to_y(pieces):
        return [pieces[0]] + [along_section(pieces[d], dy=d) for d in (1, 2, 3)]

    leave = sum_y(to_y(finish(pos, leave, low_o, high_o, (weight_z, weight_zc))))
    terms = to_y(finish(pos, stay, low_o, high_o, (weight, weight_c))) + [along_seq(leave, dz=1)]

    pieces = sum_pair(pos, terms)
    cols = sum_z([pieces[0]] + [along_section(pieces[d], dh=d) for d in (1, 2, 3)])

    rows = jnp.concatenate([cols[0], along_seq(cols[1], dc=1)], axis=1)
    rows = jnp.stack([rows] + [along_section(rows, dh=d) for d in (1, 2, 3)])
    return place(pos, [rows] + [along_section(rows, dy=d) for d in (1, 2, 3)])[None]


def solution(mesh):
    in_specs = (P("section", "seq", None),) * 6 + (P(),)
    return jax.shard_map(local, mesh=mesh, in_specs=in_specs, out_specs=P("section", None, "seq"), check_vma=False)
```

```python
import functools

import jax
import jax.numpy as jnp
from jax import lax
from jax.experimental import pallas as pl
from jax.experimental.pallas import tpu as pltpu
from jax.sharding import PartitionSpec as P

HEAD = 256
PAIR = 512
SCALE = HEAD ** -0.5
F32 = jnp.float32
BF16 = jnp.bfloat16
NT = (((1,), (1,)), ((), ()))
NN = (((1,), (0,)), ((), ()))


def seq_moves(dx, dz, dc):
    pairs = []
    for x in range(4):
        for z in range(2):
            for c in range(2):
                pairs.append((x * 4 + z * 2 + c, ((x + dx) % 4) * 4 + ((z + dz) % 2) * 2 + (c + dc) % 2))
    return pairs


def section_moves(dh, dy):
    return [(h * 4 + y, ((h + dh) % 4) * 4 + (y + dy) % 4) for h in range(4) for y in range(4)]


def along_seq(value, dx=0, dz=0, dc=0):
    return lax.ppermute(value, "seq", seq_moves(dx, dz, dc))


def along_section(value, dh=0, dy=0):
    return lax.ppermute(value, "section", section_moves(dh, dy))


def along_both(value, dh, dz):
    pairs = [(s * 16 + i, t * 16 + j) for s, t in section_moves(dh, 0) for i, j in seq_moves(0, dz, 0)]
    return lax.ppermute(value, ("section", "seq"), pairs)


def dot(a, b, dims):
    return lax.dot_general(a, b, dims, preferred_element_type=F32)


def pack_kernel(rows_ref, out_ref):
    for to in range(8):
        out_ref[to] = rows_ref[:, pl.ds(((to % 2) * 4 + to // 2) * HEAD, HEAD)]


def pack(rows):
    return pl.pallas_call(
        pack_kernel,
        out_shape=jax.ShapeDtypeStruct((8, 384, HEAD), BF16),
        in_specs=[pl.BlockSpec(memory_space=pltpu.VMEM)],
        out_specs=pl.BlockSpec(memory_space=pltpu.VMEM),
        compiler_params=pltpu.CompilerParams(vmem_limit_bytes=4 * 2**20),
        cost_estimate=pl.CostEstimate(flops=0, bytes_accessed=2**22, transcendentals=0),
        name="pack",
    )(rows)


def query_quarter(mine, other, j, first):
    source = mine if j < 2 else other
    return jnp.concatenate([source[(j % 2) * 4 + i, pl.ds(first, 64), :] for i in range(4)], axis=0)


def key_rows(mine, first, blocks):
    return jnp.concatenate([mine[i, pl.ds(first, 128), :] for i in blocks], axis=0)


def stats_kernel(m_ref, o_ref, out_ref):
    out_ref[...] = jnp.zeros_like(out_ref)
    k, v = key_rows(m_ref, 128, range(8)), key_rows(m_ref, 256, range(8))
    for j in range(4):
        spot = pl.ds(j * 256, 256)
        s = dot(k, query_quarter(m_ref, o_ref, j, 0), NT) * SCALE
        gp = dot(v, query_quarter(m_ref, o_ref, j, 64), NT)
        peak = jnp.max(s, axis=0, keepdims=True)
        p = jnp.exp(s - peak)
        out_ref[pl.ds(0, 1), spot] = peak
        out_ref[pl.ds(1, 1), spot] = jnp.sum(p, axis=0, keepdims=True)
        out_ref[pl.ds(2, 1), spot] = jnp.sum(p * gp, axis=0, keepdims=True)


def stats(mine, other):
    return pl.pallas_call(
        stats_kernel,
        out_shape=jax.ShapeDtypeStruct((8, 1024), F32),
        in_specs=[pl.BlockSpec(memory_space=pltpu.VMEM)] * 2,
        out_specs=pl.BlockSpec(memory_space=pltpu.VMEM),
        compiler_params=pltpu.CompilerParams(vmem_limit_bytes=8 * 2**20),
        cost_estimate=pl.CostEstimate(flops=10**9, bytes_accessed=2**22, transcendentals=2**20),
        name="stats",
    )(mine, other)


def grads_kernel(s0, s1, m_ref, o_ref, out, p_s, d_s, q_s, g_s):
    for j in range(4):
        q_s[pl.ds(j * 256, 256), :] = query_quarter(m_ref, o_ref, j, 0)
        g_s[pl.ds(j * 256, 256), :] = query_quarter(m_ref, o_ref, j, 64)
    for half in range(2):
        spot = pl.ds(half * 512, 512)
        blocks = range(half * 4, half * 4 + 4)
        k, v = key_rows(m_ref, 128, blocks), key_rows(m_ref, 256, blocks)
        for j in range(4):
            rows = pl.ds(j * 256, 256)
            there = pl.ds((j ^ 2) * 256, 256)
            own, far = s0[pl.ds(0, 1), rows], s1[pl.ds(0, 1), there]
            peak = jnp.maximum(own, far)
            own, far = jnp.exp(own - peak), jnp.exp(far - peak)
            total = s0[pl.ds(1, 1), rows] * own + s1[pl.ds(1, 1), there] * far
            weighted = s0[pl.ds(2, 1), rows] * own + s1[pl.ds(2, 1), there] * far
            lse = peak + jnp.log(total)
            delta = weighted / total
            s = dot(k, q_s[rows, :], NT) * SCALE
            gp = dot(v, g_s[rows, :], NT)
            p = jnp.exp(s - lse)
            p_s[:, rows] = p.astype(BF16)
            d_s[:, rows] = (p * (gp - delta)).astype(BF16)
        out[spot, pl.ds(0, HEAD)] = (dot(d_s[...], q_s[...], NN) * SCALE).astype(BF16)
        out[spot, pl.ds(HEAD, HEAD)] = dot(p_s[...], g_s[...], NN).astype(BF16)


def grads(parts, mine, other):
    return pl.pallas_call(
        grads_kernel,
        out_shape=jax.ShapeDtypeStruct((1024, 2 * HEAD), BF16),
        in_specs=[pl.BlockSpec(memory_space=pltpu.VMEM)] * 4,
        out_specs=pl.BlockSpec(memory_space=pltpu.VMEM),
        scratch_shapes=[pltpu.VMEM((512, 1024), BF16)] * 2 + [pltpu.VMEM((1024, HEAD), BF16)] * 2,
        compiler_params=pltpu.CompilerParams(vmem_limit_bytes=8 * 2**20),
        cost_estimate=pl.CostEstimate(flops=2 * 10**9, bytes_accessed=2**22, transcendentals=2**20),
        name="grads",
    )(*parts, mine, other)


def head_cols(x, d):
    return pl.ds(pl.multiple_of(lax.rem(x - d + 4, 4) * HEAD, HEAD), HEAD)


def project_kernel(pos_ref, *refs):
    blocks, weights, out = refs[:3], refs[3:5], refs[5]
    for half in range(2):
        for w, weight in enumerate(weights):
            acc = None
            for n, d in enumerate((0, 1, 3)):
                for kind in range(2):
                    block = blocks[n][pl.ds(half * 512, 512), pl.ds(kind * HEAD, HEAD)]
                    term = dot(block, weight[pl.ds(kind * 256, 256), head_cols(pos_ref[0], d)], NT)
                    acc = term if acc is None else acc + term
            out[pl.ds(half * 512, 512), pl.ds(w * 256, 256)] = acc.astype(out.dtype)


def project(pos, blocks, weights):
    return pl.pallas_call(
        project_kernel,
        out_shape=jax.ShapeDtypeStruct((1024, 512), BF16),
        in_specs=[pl.BlockSpec(memory_space=pltpu.SMEM)] + [pl.BlockSpec(memory_space=pltpu.VMEM)] * 5,
        out_specs=pl.BlockSpec(memory_space=pltpu.VMEM),
        compiler_params=pltpu.CompilerParams(vmem_limit_bytes=8 * 2**20),
        cost_estimate=pl.CostEstimate(flops=1024 * 512 * 1536 * 2, bytes_accessed=6 * 2**20, transcendentals=0),
        name="project",
    )(pos, *blocks, *weights)


def finish_kernel(pos_ref, part, low, high, w0, w1, *refs):
    outs, total = refs[:4], refs[4]
    x, y = pos_ref[0], pos_ref[1]
    for half, block in enumerate((low, high)):
        for w, weight in enumerate((w0, w1)):
            spot = (pl.ds(half * 512, 512), pl.ds(w * 256, 256))
            acc = part[spot].astype(F32)
            for kind in range(2):
                acc = acc + dot(block[:, pl.ds(kind * HEAD, HEAD)], weight[pl.ds(kind * 256, 256), head_cols(x, 2)], NT)
            total[spot] = acc.astype(BF16)
    for d, out in enumerate(outs):
        out[...] = total[pl.ds(pl.multiple_of(lax.rem(y + d, 4) * 256, 256), 256), :]


def finish(pos, part, low, high, weights):
    return pl.pallas_call(
        finish_kernel,
        out_shape=(jax.ShapeDtypeStruct((256, 512), BF16),) * 4,
        in_specs=[pl.BlockSpec(memory_space=pltpu.SMEM)] + [pl.BlockSpec(memory_space=pltpu.VMEM)] * 5,
        out_specs=(pl.BlockSpec(memory_space=pltpu.VMEM),) * 4,
        scratch_shapes=[pltpu.VMEM((1024, 512), BF16)],
        compiler_params=pltpu.CompilerParams(vmem_limit_bytes=8 * 2**20),
        cost_estimate=pl.CostEstimate(flops=1024 * 512 * 512 * 2, bytes_accessed=5 * 2**20, transcendentals=0),
        name="finish",
    )(pos, part, low, high, *weights)


def sum_y_kernel(a, b, c, d, out):
    out[...] = ((a[...].astype(F32) + b[...].astype(F32)) + (c[...].astype(F32) + d[...].astype(F32))).astype(BF16)


def sum_y(terms):
    return pl.pallas_call(
        sum_y_kernel,
        out_shape=jax.ShapeDtypeStruct((256, 512), BF16),
        in_specs=[pl.BlockSpec(memory_space=pltpu.VMEM)] * 4,
        out_specs=pl.BlockSpec(memory_space=pltpu.VMEM),
        compiler_params=pltpu.CompilerParams(vmem_limit_bytes=4 * 2**20),
        cost_estimate=pl.CostEstimate(flops=2**19, bytes_accessed=5 * 2**18, transcendentals=0),
        name="sum_y",
    )(*terms)


def sum_pair_kernel(pos_ref, *refs):
    terms, outs, total = refs[:5], refs[5:9], refs[9]
    h = pos_ref[5]
    acc = terms[0][...].astype(F32)
    for term in terms[1:]:
        acc = acc + term[...].astype(F32)
    total[...] = acc.astype(BF16)
    for d, out in enumerate(outs):
        out[...] = total[pl.ds(pl.multiple_of(lax.rem(h + d, 4) * 64, 64), 64), :]


def sum_pair(pos, terms):
    return pl.pallas_call(
        sum_pair_kernel,
        out_shape=(jax.ShapeDtypeStruct((64, 512), BF16),) * 4,
        in_specs=[pl.BlockSpec(memory_space=pltpu.SMEM)] + [pl.BlockSpec(memory_space=pltpu.VMEM)] * 5,
        out_specs=(pl.BlockSpec(memory_space=pltpu.VMEM),) * 4,
        scratch_shapes=[pltpu.VMEM((256, 512), BF16)],
        compiler_params=pltpu.CompilerParams(vmem_limit_bytes=4 * 2**20),
        cost_estimate=pl.CostEstimate(flops=2**19, bytes_accessed=5 * 2**18, transcendentals=0),
        name="sum_pair",
    )(pos, *terms)


def sum_z_kernel(a, b, c, d, *outs):
    total = ((a[...].astype(F32) + b[...].astype(F32)) + (c[...].astype(F32) + d[...].astype(F32))).astype(BF16)
    for i, out in enumerate(outs):
        out[...] = total[:, i * 256:(i + 1) * 256]


def sum_z(terms):
    return pl.pallas_call(
        sum_z_kernel,
        out_shape=(jax.ShapeDtypeStruct((64, 256), BF16),) * 2,
        in_specs=[pl.BlockSpec(memory_space=pltpu.VMEM)] * 4,
        out_specs=(pl.BlockSpec(memory_space=pltpu.VMEM),) * 2,
        compiler_params=pltpu.CompilerParams(vmem_limit_bytes=2 * 2**20),
        cost_estimate=pl.CostEstimate(flops=2**17, bytes_accessed=2**18, transcendentals=0),
        name="sum_z",
    )(*terms)


def place_kernel(pos_ref, g0, g1, g2, g3, out_ref):
    y, c, mine, h = pos_ref[1], pos_ref[3], pos_ref[4], pos_ref[5]
    for d, got in enumerate((g0, g1, g2, g3)):
        for e in range(4):
            piece = lax.rem(h - e + 4, 4)
            for i in range(2):
                at = lax.rem(y - d + 4, 4) * 512 + lax.div(piece, 2) * 256 + lax.rem(c + i, 2) * 128 + lax.rem(piece, 2) * 64
                value = got[e, :, pl.ds(i * 256, 256)]
                out_ref[pl.ds(pl.multiple_of(at, 64), 64), :] = jnp.where(mine == 1, value, jnp.zeros_like(value))


def place(pos, got):
    return pl.pallas_call(
        place_kernel,
        out_shape=jax.ShapeDtypeStruct((2048, 256), BF16),
        in_specs=[pl.BlockSpec(memory_space=pltpu.SMEM)] + [pl.BlockSpec(memory_space=pltpu.VMEM)] * 4,
        out_specs=pl.BlockSpec(memory_space=pltpu.VMEM),
        compiler_params=pltpu.CompilerParams(vmem_limit_bytes=2 * 2**20),
        cost_estimate=pl.CostEstimate(flops=0, bytes_accessed=2**21, transcendentals=0),
        name="place",
    )(pos, *got)


def local(queries, out_grad, keys, values, key_weight, value_weight, owner):
    q, g, k, v = queries[0], out_grad[0], keys[0], values[0]
    kw, vw = key_weight[0], value_weight[0]
    seq = lax.axis_index("seq")
    section = lax.axis_index("section")
    x = lax.div(seq, 4)
    h = lax.div(section, 4)
    y = lax.rem(section, 4)
    c = lax.rem(seq, 2)
    z = lax.rem(lax.div(seq, 2), 2)
    pos = jnp.stack([x, y, z, c, (section == owner[0]).astype(jnp.int32), h]).astype(jnp.int32)

    tie = lax.optimization_barrier
    rows = pack(jnp.concatenate([q, g, k, v], axis=0))
    groups = [[xx * 4 + zz * 2 + cc for xx in range(4) for zz in range(2)] for cc in range(2)]
    mine = lax.all_to_all(rows, "seq", 0, 0, axis_index_groups=groups)
    other = along_seq(mine[:, :128], dc=1)

    own = stats(mine, other)
    own, kw, vw = tie((own, kw, vw))
    parts = [own, along_seq(own, dc=1)]

    def half(matrix, at):
        return lax.dynamic_slice(matrix, (jnp.int32(0), at * 1024), (256, 1024))

    weight = jnp.concatenate([half(kw, z), half(vw, z)], axis=0)
    weight_z = along_seq(jnp.concatenate([half(kw, 1 - z), half(vw, 1 - z)], axis=0), dz=1)
    weight_c = along_seq(weight, dc=1)

    own = grads(parts, mine, other)
    right, left = along_seq(own, dx=1), along_seq(own, dx=3)
    right, left, weight_z = tie((right, left, weight_z))
    low_o, high_o = along_seq(right[:512], dx=1), along_seq(left[512:], dx=3)
    weight_zc = along_seq(weight_z, dc=1)
    blocks = (own, right, left)
    stay, leave = project(pos, blocks, (weight, weight_c)), project(pos, blocks, (weight_z, weight_zc))

    def to_y(pieces):
        return [pieces[0]] + [along_section(pieces[d], dy=d) for d in (1, 2, 3)]

    leave = sum_y(to_y(finish(pos, leave, low_o, high_o, (weight_z, weight_zc))))
    terms = to_y(finish(pos, stay, low_o, high_o, (weight, weight_c))) + [along_seq(leave, dz=1)]

    pieces = sum_pair(pos, terms)
    cols = sum_z([pieces[0]] + [along_section(pieces[d], dh=d) for d in (1, 2, 3)])

    rows = jnp.concatenate([cols[0], along_seq(cols[1], dc=1)], axis=1)
    rows = jnp.stack([rows] + [along_section(rows, dh=d) for d in (1, 2, 3)])
    return place(pos, [rows] + [along_section(rows, dy=d) for d in (1, 2, 3)])[None]


def solution(mesh):
    in_specs = (P("section", "seq", None),) * 6 + (P(),)
    return jax.shard_map(local, mesh=mesh, in_specs=in_specs, out_specs=P("section", None, "seq"), check_vma=False)
```

```python
import functools

import jax
import jax.numpy as jnp
from jax import lax
from jax.experimental import pallas as pl
from jax.experimental.pallas import tpu as pltpu
from jax.sharding import PartitionSpec as P

HEAD = 256
PAIR = 512
SCALE = HEAD ** -0.5
F32 = jnp.float32
BF16 = jnp.bfloat16
NT = (((1,), (1,)), ((), ()))
NN = (((1,), (0,)), ((), ()))


def seq_moves(dx, dz, dc):
    pairs = []
    for x in range(4):
        for z in range(2):
            for c in range(2):
                pairs.append((x * 4 + z * 2 + c, ((x + dx) % 4) * 4 + ((z + dz) % 2) * 2 + (c + dc) % 2))
    return pairs


def section_moves(dh, dy):
    return [(h * 4 + y, ((h + dh) % 4) * 4 + (y + dy) % 4) for h in range(4) for y in range(4)]


def along_seq(value, dx=0, dz=0, dc=0):
    return lax.ppermute(value, "seq", seq_moves(dx, dz, dc))


def along_section(value, dh=0, dy=0):
    return lax.ppermute(value, "section", section_moves(dh, dy))


def along_both(value, dh, dz):
    pairs = [(s * 16 + i, t * 16 + j) for s, t in section_moves(dh, 0) for i, j in seq_moves(0, dz, 0)]
    return lax.ppermute(value, ("section", "seq"), pairs)


def dot(a, b, dims):
    return lax.dot_general(a, b, dims, preferred_element_type=F32)


def pack_kernel(rows_ref, out_ref):
    for to in range(8):
        out_ref[to] = rows_ref[:, pl.ds(((to % 2) * 4 + to // 2) * HEAD, HEAD)]


def pack(rows):
    return pl.pallas_call(
        pack_kernel,
        out_shape=jax.ShapeDtypeStruct((8, 384, HEAD), BF16),
        in_specs=[pl.BlockSpec(memory_space=pltpu.VMEM)],
        out_specs=pl.BlockSpec(memory_space=pltpu.VMEM),
        compiler_params=pltpu.CompilerParams(vmem_limit_bytes=4 * 2**20),
        cost_estimate=pl.CostEstimate(flops=0, bytes_accessed=2**22, transcendentals=0),
        name="pack",
    )(rows)


def query_quarter(mine, other, j, first):
    source = mine if j < 2 else other
    return jnp.concatenate([source[(j % 2) * 4 + i, pl.ds(first, 64), :] for i in range(4)], axis=0)


def key_rows(mine, first, blocks):
    return jnp.concatenate([mine[i, pl.ds(first, 128), :] for i in blocks], axis=0)


def stats_kernel(first, m_ref, q_ref, out_ref):
    out_ref[...] = jnp.zeros_like(out_ref)
    k, v = key_rows(m_ref, 128, range(8)), key_rows(m_ref, 256, range(8))
    for j in range(2):
        spot = pl.ds(j * 256, 256)
        s = dot(k, query_quarter(m_ref, q_ref, first + j, 0), NT) * SCALE
        gp = dot(v, query_quarter(m_ref, q_ref, first + j, 64), NT)
        peak = jnp.max(s, axis=0, keepdims=True)
        p = jnp.exp(s - peak)
        out_ref[pl.ds(0, 1), spot] = peak
        out_ref[pl.ds(1, 1), spot] = jnp.sum(p, axis=0, keepdims=True)
        out_ref[pl.ds(2, 1), spot] = jnp.sum(p * gp, axis=0, keepdims=True)


def stats(first, mine, other):
    return pl.pallas_call(
        functools.partial(stats_kernel, first),
        out_shape=jax.ShapeDtypeStruct((8, 512), F32),
        in_specs=[pl.BlockSpec(memory_space=pltpu.VMEM)] * 2,
        out_specs=pl.BlockSpec(memory_space=pltpu.VMEM),
        compiler_params=pltpu.CompilerParams(vmem_limit_bytes=8 * 2**20),
        cost_estimate=pl.CostEstimate(flops=10**9, bytes_accessed=2**21, transcendentals=2**19),
        name="stats",
    )(mine, other)


def grads_kernel(a0, b0, a1, b1, m_ref, o_ref, out, p_s, d_s, q_s, g_s):
    for j in range(4):
        q_s[pl.ds(j * 256, 256), :] = query_quarter(m_ref, o_ref, j, 0)
        g_s[pl.ds(j * 256, 256), :] = query_quarter(m_ref, o_ref, j, 64)
    for half in range(2):
        spot = pl.ds(half * 512, 512)
        blocks = range(half * 4, half * 4 + 4)
        k, v = key_rows(m_ref, 128, blocks), key_rows(m_ref, 256, blocks)
        for j in range(4):
            rows = pl.ds(j * 256, 256)
            here, there = (a0, b1) if j < 2 else (b0, a1)
            part = pl.ds((j % 2) * 256, 256)
            own, far = here[pl.ds(0, 1), part], there[pl.ds(0, 1), part]
            peak = jnp.maximum(own, far)
            own, far = jnp.exp(own - peak), jnp.exp(far - peak)
            total = here[pl.ds(1, 1), part] * own + there[pl.ds(1, 1), part] * far
            weighted = here[pl.ds(2, 1), part] * own + there[pl.ds(2, 1), part] * far
            lse = peak + jnp.log(total)
            delta = weighted / total
            s = dot(k, q_s[rows, :], NT) * SCALE
            gp = dot(v, g_s[rows, :], NT)
            p = jnp.exp(s - lse)
            p_s[:, rows] = p.astype(BF16)
            d_s[:, rows] = (p * (gp - delta)).astype(BF16)
        out[spot, pl.ds(0, HEAD)] = (dot(d_s[...], q_s[...], NN) * SCALE).astype(BF16)
        out[spot, pl.ds(HEAD, HEAD)] = dot(p_s[...], g_s[...], NN).astype(BF16)


def grads(parts, mine, other):
    return pl.pallas_call(
        grads_kernel,
        out_shape=jax.ShapeDtypeStruct((1024, 2 * HEAD), BF16),
        in_specs=[pl.BlockSpec(memory_space=pltpu.VMEM)] * 6,
        out_specs=pl.BlockSpec(memory_space=pltpu.VMEM),
        scratch_shapes=[pltpu.VMEM((512, 1024), BF16)] * 2 + [pltpu.VMEM((1024, HEAD), BF16)] * 2,
        compiler_params=pltpu.CompilerParams(vmem_limit_bytes=8 * 2**20),
        cost_estimate=pl.CostEstimate(flops=2 * 10**9, bytes_accessed=2**22, transcendentals=2**20),
        name="grads",
    )(*parts, mine, other)


def head_cols(x, d):
    return pl.ds(pl.multiple_of(lax.rem(x - d + 4, 4) * HEAD, HEAD), HEAD)


def project_kernel(pos_ref, *refs):
    blocks, weights, out = refs[:3], refs[3:5], refs[5]
    for half in range(2):
        for w, weight in enumerate(weights):
            acc = None
            for n, d in enumerate((0, 1, 3)):
                for kind in range(2):
                    block = blocks[n][pl.ds(half * 512, 512), pl.ds(kind * HEAD, HEAD)]
                    term = dot(block, weight[pl.ds(kind * 256, 256), head_cols(pos_ref[0], d)], NT)
                    acc = term if acc is None else acc + term
            out[pl.ds(half * 512, 512), pl.ds(w * 256, 256)] = acc.astype(out.dtype)


def project(pos, blocks, weights):
    return pl.pallas_call(
        project_kernel,
        out_shape=jax.ShapeDtypeStruct((1024, 512), BF16),
        in_specs=[pl.BlockSpec(memory_space=pltpu.SMEM)] + [pl.BlockSpec(memory_space=pltpu.VMEM)] * 5,
        out_specs=pl.BlockSpec(memory_space=pltpu.VMEM),
        compiler_params=pltpu.CompilerParams(vmem_limit_bytes=8 * 2**20),
        cost_estimate=pl.CostEstimate(flops=1024 * 512 * 1536 * 2, bytes_accessed=6 * 2**20, transcendentals=0),
        name="project",
    )(pos, *blocks, *weights)


def finish_kernel(pos_ref, part, low, high, w0, w1, *refs):
    outs, total = refs[:4], refs[4]
    x, y = pos_ref[0], pos_ref[1]
    for half, block in enumerate((low, high)):
        for w, weight in enumerate((w0, w1)):
            spot = (pl.ds(half * 512, 512), pl.ds(w * 256, 256))
            acc = part[spot].astype(F32)
            for kind in range(2):
                acc = acc + dot(block[:, pl.ds(kind * HEAD, HEAD)], weight[pl.ds(kind * 256, 256), head_cols(x, 2)], NT)
            total[spot] = acc.astype(BF16)
    for d, out in enumerate(outs):
        out[...] = total[pl.ds(pl.multiple_of(lax.rem(y + d, 4) * 256, 256), 256), :]


def finish(pos, part, low, high, weights):
    return pl.pallas_call(
        finish_kernel,
        out_shape=(jax.ShapeDtypeStruct((256, 512), BF16),) * 4,
        in_specs=[pl.BlockSpec(memory_space=pltpu.SMEM)] + [pl.BlockSpec(memory_space=pltpu.VMEM)] * 5,
        out_specs=(pl.BlockSpec(memory_space=pltpu.VMEM),) * 4,
        scratch_shapes=[pltpu.VMEM((1024, 512), BF16)],
        compiler_params=pltpu.CompilerParams(vmem_limit_bytes=8 * 2**20),
        cost_estimate=pl.CostEstimate(flops=1024 * 512 * 512 * 2, bytes_accessed=5 * 2**20, transcendentals=0),
        name="finish",
    )(pos, part, low, high, *weights)


def sum_y_kernel(a, b, c, d, out):
    out[...] = ((a[...].astype(F32) + b[...].astype(F32)) + (c[...].astype(F32) + d[...].astype(F32))).astype(BF16)


def sum_y(terms):
    return pl.pallas_call(
        sum_y_kernel,
        out_shape=jax.ShapeDtypeStruct((256, 512), BF16),
        in_specs=[pl.BlockSpec(memory_space=pltpu.VMEM)] * 4,
        out_specs=pl.BlockSpec(memory_space=pltpu.VMEM),
        compiler_params=pltpu.CompilerParams(vmem_limit_bytes=4 * 2**20),
        cost_estimate=pl.CostEstimate(flops=2**19, bytes_accessed=5 * 2**18, transcendentals=0),
        name="sum_y",
    )(*terms)


def sum_pair_kernel(pos_ref, *refs):
    terms, outs, total = refs[:5], refs[5:9], refs[9]
    h = pos_ref[5]
    acc = terms[0][...].astype(F32)
    for term in terms[1:]:
        acc = acc + term[...].astype(F32)
    total[...] = acc.astype(BF16)
    for d, out in enumerate(outs):
        out[...] = total[pl.ds(pl.multiple_of(lax.rem(h + d, 4) * 64, 64), 64), :]


def sum_pair(pos, terms):
    return pl.pallas_call(
        sum_pair_kernel,
        out_shape=(jax.ShapeDtypeStruct((64, 512), BF16),) * 4,
        in_specs=[pl.BlockSpec(memory_space=pltpu.SMEM)] + [pl.BlockSpec(memory_space=pltpu.VMEM)] * 5,
        out_specs=(pl.BlockSpec(memory_space=pltpu.VMEM),) * 4,
        scratch_shapes=[pltpu.VMEM((256, 512), BF16)],
        compiler_params=pltpu.CompilerParams(vmem_limit_bytes=4 * 2**20),
        cost_estimate=pl.CostEstimate(flops=2**19, bytes_accessed=5 * 2**18, transcendentals=0),
        name="sum_pair",
    )(pos, *terms)


def sum_z_kernel(a, b, c, d, *outs):
    total = ((a[...].astype(F32) + b[...].astype(F32)) + (c[...].astype(F32) + d[...].astype(F32))).astype(BF16)
    for i, out in enumerate(outs):
        out[...] = total[:, i * 256:(i + 1) * 256]


def sum_z(terms):
    return pl.pallas_call(
        sum_z_kernel,
        out_shape=(jax.ShapeDtypeStruct((64, 256), BF16),) * 2,
        in_specs=[pl.BlockSpec(memory_space=pltpu.VMEM)] * 4,
        out_specs=(pl.BlockSpec(memory_space=pltpu.VMEM),) * 2,
        compiler_params=pltpu.CompilerParams(vmem_limit_bytes=2 * 2**20),
        cost_estimate=pl.CostEstimate(flops=2**17, bytes_accessed=2**18, transcendentals=0),
        name="sum_z",
    )(*terms)


def place_kernel(pos_ref, g0, g1, g2, g3, out_ref):
    y, c, mine, h = pos_ref[1], pos_ref[3], pos_ref[4], pos_ref[5]
    for d, got in enumerate((g0, g1, g2, g3)):
        for e in range(4):
            piece = lax.rem(h - e + 4, 4)
            for i in range(2):
                at = lax.rem(y - d + 4, 4) * 512 + lax.div(piece, 2) * 256 + lax.rem(c + i, 2) * 128 + lax.rem(piece, 2) * 64
                value = got[e, :, pl.ds(i * 256, 256)]
                out_ref[pl.ds(pl.multiple_of(at, 64), 64), :] = jnp.where(mine == 1, value, jnp.zeros_like(value))


def place(pos, got):
    return pl.pallas_call(
        place_kernel,
        out_shape=jax.ShapeDtypeStruct((2048, 256), BF16),
        in_specs=[pl.BlockSpec(memory_space=pltpu.SMEM)] + [pl.BlockSpec(memory_space=pltpu.VMEM)] * 4,
        out_specs=pl.BlockSpec(memory_space=pltpu.VMEM),
        compiler_params=pltpu.CompilerParams(vmem_limit_bytes=2 * 2**20),
        cost_estimate=pl.CostEstimate(flops=0, bytes_accessed=2**21, transcendentals=0),
        name="place",
    )(pos, *got)


def local(queries, out_grad, keys, values, key_weight, value_weight, owner):
    q, g, k, v = queries[0], out_grad[0], keys[0], values[0]
    kw, vw = key_weight[0], value_weight[0]
    seq = lax.axis_index("seq")
    section = lax.axis_index("section")
    x = lax.div(seq, 4)
    h = lax.div(section, 4)
    y = lax.rem(section, 4)
    c = lax.rem(seq, 2)
    z = lax.rem(lax.div(seq, 2), 2)
    pos = jnp.stack([x, y, z, c, (section == owner[0]).astype(jnp.int32), h]).astype(jnp.int32)

    tie = lax.optimization_barrier
    rows = pack(jnp.concatenate([q, g, k, v], axis=0))
    groups = [[xx * 4 + zz * 2 + cc for xx in range(4) for zz in range(2)] for cc in range(2)]
    mine = lax.all_to_all(rows, "seq", 0, 0, axis_index_groups=groups)
    other = along_seq(mine[:, :128], dc=1)

    first, second = stats(0, mine, mine), stats(2, mine, other)
    second, kw, vw = tie((second, kw, vw))
    parts = [first, second, along_seq(first, dc=1), along_seq(second, dc=1)]

    def half(matrix, at):
        return lax.dynamic_slice(matrix, (jnp.int32(0), at * 1024), (256, 1024))

    weight = jnp.concatenate([half(kw, z), half(vw, z)], axis=0)
    weight_z = along_seq(jnp.concatenate([half(kw, 1 - z), half(vw, 1 - z)], axis=0), dz=1)
    weight_c = along_seq(weight, dc=1)

    own = grads(parts, mine, other)
    right, left = along_seq(own, dx=1), along_seq(own, dx=3)
    right, left, weight_z = tie((right, left, weight_z))
    low_o, high_o = along_seq(right[:512], dx=1), along_seq(left[512:], dx=3)
    weight_zc = along_seq(weight_z, dc=1)
    blocks = (own, right, left)
    stay, leave = project(pos, blocks, (weight, weight_c)), project(pos, blocks, (weight_z, weight_zc))

    def to_y(pieces):
        return [pieces[0]] + [along_section(pieces[d], dy=d) for d in (1, 2, 3)]

    leave = sum_y(to_y(finish(pos, leave, low_o, high_o, (weight_z, weight_zc))))
    terms = to_y(finish(pos, stay, low_o, high_o, (weight, weight_c))) + [along_seq(leave, dz=1)]

    pieces = sum_pair(pos, terms)
    cols = sum_z([pieces[0]] + [along_section(pieces[d], dh=d) for d in (1, 2, 3)])

    rows = jnp.concatenate([cols[0], along_seq(cols[1], dc=1)], axis=1)
    rows = jnp.stack([rows] + [along_section(rows, dh=d) for d in (1, 2, 3)])
    return place(pos, [rows] + [along_section(rows, dy=d) for d in (1, 2, 3)])[None]


def solution(mesh):
    in_specs = (P("section", "seq", None),) * 6 + (P(),)
    return jax.shard_map(local, mesh=mesh, in_specs=in_specs, out_specs=P("section", None, "seq"), check_vma=False)
```

```python
import functools

import jax
import jax.numpy as jnp
from jax import lax
from jax.experimental import pallas as pl
from jax.experimental.pallas import tpu as pltpu
from jax.sharding import PartitionSpec as P

HEAD = 256
PAIR = 512
SCALE = HEAD ** -0.5
F32 = jnp.float32
BF16 = jnp.bfloat16
NT = (((1,), (1,)), ((), ()))
NN = (((1,), (0,)), ((), ()))


def seq_moves(dx, dz, dc):
    pairs = []
    for x in range(4):
        for z in range(2):
            for c in range(2):
                pairs.append((x * 4 + z * 2 + c, ((x + dx) % 4) * 4 + ((z + dz) % 2) * 2 + (c + dc) % 2))
    return pairs


def section_moves(dh, dy):
    return [(h * 4 + y, ((h + dh) % 4) * 4 + (y + dy) % 4) for h in range(4) for y in range(4)]


def along_seq(value, dx=0, dz=0, dc=0):
    return lax.ppermute(value, "seq", seq_moves(dx, dz, dc))


def along_section(value, dh=0, dy=0):
    return lax.ppermute(value, "section", section_moves(dh, dy))


def along_both(value, dh, dz):
    pairs = [(s * 16 + i, t * 16 + j) for s, t in section_moves(dh, 0) for i, j in seq_moves(0, dz, 0)]
    return lax.ppermute(value, ("section", "seq"), pairs)


def dot(a, b, dims):
    return lax.dot_general(a, b, dims, preferred_element_type=F32)


def pack_kernel(rows_ref, out_ref):
    for to in range(8):
        out_ref[to] = rows_ref[:, pl.ds(((to % 2) * 4 + to // 2) * HEAD, HEAD)]


def pack(rows):
    return pl.pallas_call(
        pack_kernel,
        out_shape=jax.ShapeDtypeStruct((8, 384, HEAD), BF16),
        in_specs=[pl.BlockSpec(memory_space=pltpu.VMEM)],
        out_specs=pl.BlockSpec(memory_space=pltpu.VMEM),
        compiler_params=pltpu.CompilerParams(vmem_limit_bytes=4 * 2**20),
        cost_estimate=pl.CostEstimate(flops=0, bytes_accessed=2**22, transcendentals=0),
        name="pack",
    )(rows)


def query_quarter(mine, other, j, first):
    source = mine if j < 2 else other
    return jnp.concatenate([source[(j % 2) * 4 + i, pl.ds(first, 64), :] for i in range(4)], axis=0)


def key_rows(mine, first, blocks):
    return jnp.concatenate([mine[i, pl.ds(first, 128), :] for i in blocks], axis=0)


def stats_kernel(first, m_ref, q_ref, out_ref):
    out_ref[...] = jnp.zeros_like(out_ref)
    k, v = key_rows(m_ref, 128, range(8)), key_rows(m_ref, 256, range(8))
    for j in range(2):
        spot = pl.ds(j * 256, 256)
        s = dot(k, query_quarter(m_ref, q_ref, first + j, 0), NT) * SCALE
        gp = dot(v, query_quarter(m_ref, q_ref, first + j, 64), NT)
        peak = jnp.max(s, axis=0, keepdims=True)
        p = jnp.exp(s - peak)
        out_ref[pl.ds(0, 1), spot] = peak
        out_ref[pl.ds(1, 1), spot] = jnp.sum(p, axis=0, keepdims=True)
        out_ref[pl.ds(2, 1), spot] = jnp.sum(p * gp, axis=0, keepdims=True)


def stats(first, mine, other):
    return pl.pallas_call(
        functools.partial(stats_kernel, first),
        out_shape=jax.ShapeDtypeStruct((8, 512), F32),
        in_specs=[pl.BlockSpec(memory_space=pltpu.VMEM)] * 2,
        out_specs=pl.BlockSpec(memory_space=pltpu.VMEM),
        compiler_params=pltpu.CompilerParams(vmem_limit_bytes=8 * 2**20),
        cost_estimate=pl.CostEstimate(flops=10**9, bytes_accessed=2**21, transcendentals=2**19),
        name="stats",
    )(mine, other)


def grads_kernel(a0, b0, a1, b1, m_ref, o_ref, out, p_s, d_s, q_s, g_s):
    for j in range(4):
        q_s[pl.ds(j * 256, 256), :] = query_quarter(m_ref, o_ref, j, 0)
        g_s[pl.ds(j * 256, 256), :] = query_quarter(m_ref, o_ref, j, 64)
    for half in range(2):
        spot = pl.ds(half * 512, 512)
        blocks = range(half * 4, half * 4 + 4)
        k, v = key_rows(m_ref, 128, blocks), key_rows(m_ref, 256, blocks)
        for j in range(4):
            rows = pl.ds(j * 256, 256)
            here, there = (a0, b1) if j < 2 else (b0, a1)
            part = pl.ds((j % 2) * 256, 256)
            own, far = here[pl.ds(0, 1), part], there[pl.ds(0, 1), part]
            peak = jnp.maximum(own, far)
            own, far = jnp.exp(own - peak), jnp.exp(far - peak)
            total = here[pl.ds(1, 1), part] * own + there[pl.ds(1, 1), part] * far
            weighted = here[pl.ds(2, 1), part] * own + there[pl.ds(2, 1), part] * far
            lse = peak + jnp.log(total)
            delta = weighted / total
            s = dot(k, q_s[rows, :], NT) * SCALE
            gp = dot(v, g_s[rows, :], NT)
            p = jnp.exp(s - lse)
            p_s[:, rows] = p.astype(BF16)
            d_s[:, rows] = (p * (gp - delta)).astype(BF16)
        out[spot, pl.ds(0, HEAD)] = (dot(d_s[...], q_s[...], NN) * SCALE).astype(BF16)
        out[spot, pl.ds(HEAD, HEAD)] = dot(p_s[...], g_s[...], NN).astype(BF16)


def grads(parts, mine, other):
    return pl.pallas_call(
        grads_kernel,
        out_shape=jax.ShapeDtypeStruct((1024, 2 * HEAD), BF16),
        in_specs=[pl.BlockSpec(memory_space=pltpu.VMEM)] * 6,
        out_specs=pl.BlockSpec(memory_space=pltpu.VMEM),
        scratch_shapes=[pltpu.VMEM((512, 1024), BF16)] * 2 + [pltpu.VMEM((1024, HEAD), BF16)] * 2,
        compiler_params=pltpu.CompilerParams(vmem_limit_bytes=8 * 2**20),
        cost_estimate=pl.CostEstimate(flops=2 * 10**9, bytes_accessed=2**22, transcendentals=2**20),
        name="grads",
    )(*parts, mine, other)


def head_cols(x, d):
    return pl.ds(pl.multiple_of(lax.rem(x - d + 4, 4) * HEAD, HEAD), HEAD)


def project_kernel(pos_ref, *refs):
    blocks, weights, outs = refs[:3], refs[3:7], refs[7:]
    for half in range(2):
        for w, weight in enumerate(weights):
            acc = None
            for n, d in enumerate((0, 1, 3)):
                for kind in range(2):
                    block = blocks[n][pl.ds(half * 512, 512), pl.ds(kind * HEAD, HEAD)]
                    term = dot(block, weight[pl.ds(kind * 256, 256), head_cols(pos_ref[0], d)], NT)
                    acc = term if acc is None else acc + term
            outs[w // 2][pl.ds(half * 512, 512), pl.ds((w % 2) * 256, 256)] = acc.astype(BF16)


def project(pos, blocks, weights):
    return pl.pallas_call(
        project_kernel,
        out_shape=(jax.ShapeDtypeStruct((1024, 512), BF16),) * 2,
        in_specs=[pl.BlockSpec(memory_space=pltpu.SMEM)] + [pl.BlockSpec(memory_space=pltpu.VMEM)] * 7,
        out_specs=(pl.BlockSpec(memory_space=pltpu.VMEM),) * 2,
        compiler_params=pltpu.CompilerParams(vmem_limit_bytes=10 * 2**20),
        cost_estimate=pl.CostEstimate(flops=1024 * 1024 * 1536 * 2, bytes_accessed=9 * 2**20, transcendentals=0),
        name="project",
    )(pos, *blocks, *weights)


def finish_kernel(pos_ref, part, low, high, w0, w1, *refs):
    outs, total = refs[:4], refs[4]
    x, y = pos_ref[0], pos_ref[1]
    for half, block in enumerate((low, high)):
        for w, weight in enumerate((w0, w1)):
            spot = (pl.ds(half * 512, 512), pl.ds(w * 256, 256))
            acc = part[spot].astype(F32)
            for kind in range(2):
                acc = acc + dot(block[:, pl.ds(kind * HEAD, HEAD)], weight[pl.ds(kind * 256, 256), head_cols(x, 2)], NT)
            total[spot] = acc.astype(BF16)
    for d, out in enumerate(outs):
        out[...] = total[pl.ds(pl.multiple_of(lax.rem(y + d, 4) * 256, 256), 256), :]


def finish(pos, part, low, high, weights):
    return pl.pallas_call(
        finish_kernel,
        out_shape=(jax.ShapeDtypeStruct((256, 512), BF16),) * 4,
        in_specs=[pl.BlockSpec(memory_space=pltpu.SMEM)] + [pl.BlockSpec(memory_space=pltpu.VMEM)] * 5,
        out_specs=(pl.BlockSpec(memory_space=pltpu.VMEM),) * 4,
        scratch_shapes=[pltpu.VMEM((1024, 512), BF16)],
        compiler_params=pltpu.CompilerParams(vmem_limit_bytes=8 * 2**20),
        cost_estimate=pl.CostEstimate(flops=1024 * 512 * 512 * 2, bytes_accessed=5 * 2**20, transcendentals=0),
        name="finish",
    )(pos, part, low, high, *weights)


def sum_y_kernel(a, b, c, d, out):
    out[...] = ((a[...].astype(F32) + b[...].astype(F32)) + (c[...].astype(F32) + d[...].astype(F32))).astype(BF16)


def sum_y(terms):
    return pl.pallas_call(
        sum_y_kernel,
        out_shape=jax.ShapeDtypeStruct((256, 512), BF16),
        in_specs=[pl.BlockSpec(memory_space=pltpu.VMEM)] * 4,
        out_specs=pl.BlockSpec(memory_space=pltpu.VMEM),
        compiler_params=pltpu.CompilerParams(vmem_limit_bytes=4 * 2**20),
        cost_estimate=pl.CostEstimate(flops=2**19, bytes_accessed=5 * 2**18, transcendentals=0),
        name="sum_y",
    )(*terms)


def sum_pair_kernel(pos_ref, *refs):
    terms, outs, total = refs[:5], refs[5:9], refs[9]
    h = pos_ref[5]
    acc = terms[0][...].astype(F32)
    for term in terms[1:]:
        acc = acc + term[...].astype(F32)
    total[...] = acc.astype(BF16)
    for d, out in enumerate(outs):
        out[...] = total[pl.ds(pl.multiple_of(lax.rem(h + d, 4) * 64, 64), 64), :]


def sum_pair(pos, terms):
    return pl.pallas_call(
        sum_pair_kernel,
        out_shape=(jax.ShapeDtypeStruct((64, 512), BF16),) * 4,
        in_specs=[pl.BlockSpec(memory_space=pltpu.SMEM)] + [pl.BlockSpec(memory_space=pltpu.VMEM)] * 5,
        out_specs=(pl.BlockSpec(memory_space=pltpu.VMEM),) * 4,
        scratch_shapes=[pltpu.VMEM((256, 512), BF16)],
        compiler_params=pltpu.CompilerParams(vmem_limit_bytes=4 * 2**20),
        cost_estimate=pl.CostEstimate(flops=2**19, bytes_accessed=5 * 2**18, transcendentals=0),
        name="sum_pair",
    )(pos, *terms)


def sum_z_kernel(a, b, c, d, *outs):
    total = ((a[...].astype(F32) + b[...].astype(F32)) + (c[...].astype(F32) + d[...].astype(F32))).astype(BF16)
    for i, out in enumerate(outs):
        out[...] = total[:, i * 256:(i + 1) * 256]


def sum_z(terms):
    return pl.pallas_call(
        sum_z_kernel,
        out_shape=(jax.ShapeDtypeStruct((64, 256), BF16),) * 2,
        in_specs=[pl.BlockSpec(memory_space=pltpu.VMEM)] * 4,
        out_specs=(pl.BlockSpec(memory_space=pltpu.VMEM),) * 2,
        compiler_params=pltpu.CompilerParams(vmem_limit_bytes=2 * 2**20),
        cost_estimate=pl.CostEstimate(flops=2**17, bytes_accessed=2**18, transcendentals=0),
        name="sum_z",
    )(*terms)


def place_kernel(pos_ref, g0, g1, g2, g3, out_ref):
    y, c, mine, h = pos_ref[1], pos_ref[3], pos_ref[4], pos_ref[5]
    for d, got in enumerate((g0, g1, g2, g3)):
        for e in range(4):
            piece = lax.rem(h - e + 4, 4)
            for i in range(2):
                at = lax.rem(y - d + 4, 4) * 512 + lax.div(piece, 2) * 256 + lax.rem(c + i, 2) * 128 + lax.rem(piece, 2) * 64
                value = got[e, :, pl.ds(i * 256, 256)]
                out_ref[pl.ds(pl.multiple_of(at, 64), 64), :] = jnp.where(mine == 1, value, jnp.zeros_like(value))


def place(pos, got):
    return pl.pallas_call(
        place_kernel,
        out_shape=jax.ShapeDtypeStruct((2048, 256), BF16),
        in_specs=[pl.BlockSpec(memory_space=pltpu.SMEM)] + [pl.BlockSpec(memory_space=pltpu.VMEM)] * 4,
        out_specs=pl.BlockSpec(memory_space=pltpu.VMEM),
        compiler_params=pltpu.CompilerParams(vmem_limit_bytes=2 * 2**20),
        cost_estimate=pl.CostEstimate(flops=0, bytes_accessed=2**21, transcendentals=0),
        name="place",
    )(pos, *got)


def local(queries, out_grad, keys, values, key_weight, value_weight, owner):
    q, g, k, v = queries[0], out_grad[0], keys[0], values[0]
    kw, vw = key_weight[0], value_weight[0]
    seq = lax.axis_index("seq")
    section = lax.axis_index("section")
    x = lax.div(seq, 4)
    h = lax.div(section, 4)
    y = lax.rem(section, 4)
    c = lax.rem(seq, 2)
    z = lax.rem(lax.div(seq, 2), 2)
    pos = jnp.stack([x, y, z, c, (section == owner[0]).astype(jnp.int32), h]).astype(jnp.int32)

    tie = lax.optimization_barrier
    rows = pack(jnp.concatenate([q, g, k, v], axis=0))
    groups = [[xx * 4 + zz * 2 + cc for xx in range(4) for zz in range(2)] for cc in range(2)]
    mine = lax.all_to_all(rows, "seq", 0, 0, axis_index_groups=groups)
    other = along_seq(mine[:, :128], dc=1)

    first, second = stats(0, mine, mine), stats(2, mine, other)
    second, kw, vw = tie((second, kw, vw))
    parts = [first, second, along_seq(first, dc=1), along_seq(second, dc=1)]

    def half(matrix, at):
        return lax.dynamic_slice(matrix, (jnp.int32(0), at * 1024), (256, 1024))

    weight = jnp.concatenate([half(kw, z), half(vw, z)], axis=0)
    weight_z = along_seq(jnp.concatenate([half(kw, 1 - z), half(vw, 1 - z)], axis=0), dz=1)
    weight_c = along_seq(weight, dc=1)

    own = grads(parts, mine, other)
    right, left = along_seq(own, dx=1), along_seq(own, dx=3)
    low_r, high_l, weight_z = tie((right[:512], left[512:], weight_z))
    low_o, high_o = along_seq(low_r, dx=1), along_seq(high_l, dx=3)
    weight_zc = along_seq(weight_z, dc=1)
    blocks = (own, right, left)
    stay, leave = project(pos, blocks, (weight, weight_c, weight_z, weight_zc))

    def to_y(pieces):
        return [pieces[0]] + [along_section(pieces[d], dy=d) for d in (1, 2, 3)]

    leave = sum_y(to_y(finish(pos, leave, low_o, high_o, (weight_z, weight_zc))))
    terms = to_y(finish(pos, stay, low_o, high_o, (weight, weight_c))) + [along_seq(leave, dz=1)]

    pieces = sum_pair(pos, terms)
    cols = sum_z([pieces[0]] + [along_section(pieces[d], dh=d) for d in (1, 2, 3)])

    rows = jnp.concatenate([cols[0], along_seq(cols[1], dc=1)], axis=1)
    rows = jnp.stack([rows] + [along_section(rows, dh=d) for d in (1, 2, 3)])
    return place(pos, [rows] + [along_section(rows, dy=d) for d in (1, 2, 3)])[None]


def solution(mesh):
    in_specs = (P("section", "seq", None),) * 6 + (P(),)
    return jax.shard_map(local, mesh=mesh, in_specs=in_specs, out_specs=P("section", None, "seq"), check_vma=False)
```
